128 devices in a mesh: col: 16 (over x, y), obs: 8 (over z, core).
Axes of the slice: x: 4, y: 4, z: 4, core: 2. Of those that a mesh axis runs over, the one named last changes fastest.
Arguments:
- departures: float32 [16384, 4096], P(('col', 'obs')), may hold values from -6 to 6
- obs_owner: int32 [16384, 1], P(('col', 'obs')), may hold values from 0 to 127; in each aligned block of 128 rows (0 to 127, 128 to 255, ...) at most 2 rows name the same one
- obs_column: int32 [16384], P(('col', 'obs')), may hold values from 0 to 1023
- obs_count: int32 [128], P(('col', 'obs')), may hold values from 64 to 128, as said below
- channel_count: int32 [8], P('obs'), may hold values from 256 to 4096, as said below
- error_inv: float32 [8, 4096], P('obs'), may hold values from 0.25 to 4
- jacobian: bfloat16 [8, 548, 4096], P('obs'), may hold values from -0.25 to 0.25
- vertical: float32 [4, 137, 137], replicated, may hold values from -0.5 to 0.5
Outputs:
- increment: float32 [4, 137, 131072], P(None, None, ('col', 'obs'))
- residual: float32 [4, 137, 131072], P(None, None, ('col', 'obs'))
The draws below stay inside these ranges and needn't reach their ends.
Inputs may be any that keep to these rules, and one draw needn't show every extreme that they name: `obs_owner`: within the rows of one device (aligned blocks of 128 rows) no owner is named by more than 2 rows; in some block some owner is named by exactly 2. `obs_count`: some device uses all 128 slots. `channel_count`: some swath uses all 4096 channels.
All inputs are finite; a program needn't handle non-finite values.
Results may differ from the reference program's by a relative error of at most 0.017.
Values may be sent and summed in bfloat16 or wider, within the bound.
A program may use at most 64 MiB of HBM per device.

```python
import math
import jax
import jax.numpy as jnp
import numpy as np
from jax import lax

NVAR = 4
LEV = 137
CH = 4096
COLS_DEV = 1024
NOBS_DEV = 128
ITERS = 2
CAP = 2
OBS = 16384
N_OBS = 8
DEVICES = 128


def draw_obs_count(key, part):
    key = jax.random.fold_in(key, 11)
    key_counts, key_pick = jax.random.split(key)
    counts = jax.random.randint(key_counts, (DEVICES,), NOBS_DEV // 2, NOBS_DEV + 1, dtype=jnp.int32)
    chosen = jax.random.randint(key_pick, (), 0, DEVICES, dtype=jnp.int32)
    return jnp.where(jnp.arange(DEVICES, dtype=jnp.int32) == chosen, NOBS_DEV, counts).astype(jnp.int32)


def draw_channel_count(key, part):
    key = jax.random.fold_in(key, 23)
    key_counts, key_pick = jax.random.split(key)
    counts = jax.random.randint(key_counts, (N_OBS,), CH // 16, CH + 1, dtype=jnp.int32)
    chosen = jax.random.randint(key_pick, (), 0, N_OBS, dtype=jnp.int32)
    return jnp.where(jnp.arange(N_OBS, dtype=jnp.int32) == chosen, CH, counts).astype(jnp.int32)


def plant(drawn, key, least, high):
    dims = drawn.shape
    place = [jax.random.randint(jax.random.fold_in(key, axis), (), 0, dims[axis]) for axis in range(len(dims))]
    drawn = drawn.at[tuple(place)].set(least)
    longest = dims.index(max(dims))
    place[longest] = (place[longest] + 1) % dims[longest]
    return drawn.at[tuple(place)].set(high)


def block_levels(key, dims, cuts, low, largest):
    factor_of, own = 1.0, jax.random.fold_in(key, 6)
    for axis_at, shards_of in cuts:
        steps = jnp.exp(jax.random.uniform(jax.random.fold_in(own, axis_at), (shards_of,), jnp.float32, low / len(cuts), largest / len(cuts)))
        factor_of = factor_of * jnp.repeat(steps, dims[axis_at] // shards_of).reshape([-1 if axis == axis_at else 1 for axis in range(len(dims))])
    return factor_of


def assign_block(own_key, own, number, rows, amount, top, limit, slope):
    sequence = jax.random.permutation(own_key, amount)
    heavy_load, ordinary = shares(amount, rows * top, limit, slope, True), shares(amount, rows * top, limit, slope, False)
    places = jnp.arange(amount)

    def named(sizes, offset_by):
        used = int((sizes > 0).sum())
        fixed = max(1, used // 4)
        moved = fixed + (places - fixed + offset_by * (used - fixed)) % max(1, amount - fixed)
        return jnp.zeros((amount,), jnp.int32).at[sequence[jnp.where(places < fixed, places, moved)]].set(jnp.asarray(sizes, jnp.int32))

    sizes = jnp.where(number % 4 == 0, named(heavy_load, number // 4), named(ordinary, number - number // 4 - 1))
    mixed = jax.random.permutation(jax.random.fold_in(own, 3), amount)
    source_of, sink = mixed[0:amount // 2 * 2:2], mixed[1:amount // 2 * 2:2]
    room = jnp.minimum(sizes[source_of] - 1, limit - sizes[sink]) // 2
    room = jnp.where((source_of == sequence[0]) | (sink == sequence[0]) | (sizes[sink] == 0), 0, jnp.maximum(room, 0))
    moved = jax.random.randint(jax.random.fold_in(own, 4), (amount // 2,), 0, 1 << 20) % (room + 1)
    sizes = sizes.at[source_of].add(-moved).at[sink].add(moved)
    members = jnp.searchsorted(jnp.cumsum(sizes), jnp.arange(rows * top), side="right").astype(jnp.int32)
    table = members.reshape(top, rows).T
    table = table[jax.random.permutation(jax.random.fold_in(own, 1), rows)]
    offset_by = jax.random.randint(jax.random.fold_in(own, 2), (rows, 1), 0, top)
    return jnp.take_along_axis(table, (jnp.arange(top)[None, :] + offset_by) % top, axis=1)


def shares(count, total, most, skew, full):
    portions = [(1 << 20) // math.isqrt(rank ** skew) + 1 for rank in range(1, count + 1)]
    largest = most if full else min(most, max(-(-total // count), total * portions[0] // sum(portions)))
    least = 1 if total - largest >= count - 1 else 0
    given, surplus = [largest] + [least] * (count - 1), total - largest - least * (count - 1)
    while surplus > 0:
        movable = [i for i in range(1, count) if given[i] < largest] or [i for i in range(1, count) if given[i] < most]
        mass, left = sum([portions[i] for i in movable]), surplus
        for i in movable:
            extra = min(most - given[i], max(1, left * portions[i] // mass), surplus)
            given[i] = given[i] + extra
            surplus = surplus - extra
    return np.array(given)


def normal_values(rng, extent, deviation, limit, cuts=(), held_as=jnp.bfloat16):
    array = jax.random.normal(rng, extent, jnp.float32) * deviation
    if len(cuts) > 0:
        array = block_levels(rng, extent, cuts, -0.22, 0.18) * array
    return jnp.clip(array, min=-limit, max=limit).astype(held_as)


def setup_inputs(seed: int = 0) -> dict:
    arg_keys = jax.random.split(jax.random.key(seed), 9)
    departures = normal_values(arg_keys[0], (OBS, CH), 1.0, 6.0, ((0, 128),), jnp.float32)
    obs_owner_keys = jax.random.split(jax.random.fold_in(arg_keys[1], 1), OBS // NOBS_DEV)
    obs_owner_turns = jax.random.permutation(jax.random.fold_in(arg_keys[1], 3), OBS // NOBS_DEV)
    obs_owner = jax.vmap(lambda own, number: assign_block(jax.random.fold_in(arg_keys[1], 2), own, number, NOBS_DEV, DEVICES, 1, CAP, 1))(obs_owner_keys, obs_owner_turns).reshape((OBS, 1))
    obs_column = plant(jax.random.randint(arg_keys[2], (OBS,), 0, COLS_DEV), jax.random.fold_in(arg_keys[2], 1), 0, COLS_DEV - 1).astype(jnp.int32)
    obs_count = draw_obs_count(jax.random.fold_in(arg_keys[8], 71), 0)
    channel_count = draw_channel_count(jax.random.fold_in(arg_keys[8], 71), 0)
    error_inv = jnp.clip(jnp.exp(math.log(4.0) - 2.7725887 * jax.random.uniform(arg_keys[5], (N_OBS, CH), jnp.float32) ** block_levels(arg_keys[5], (N_OBS, CH), ((0, 8),), -0.2, 0.2)), 0.25, 4.0)
    jacobian = normal_values(arg_keys[6], (N_OBS, NVAR * LEV, CH), (NVAR * LEV) ** -0.5, 0.25, ((0, 8),))
    vertical = normal_values(arg_keys[7], (NVAR, LEV, LEV), LEV ** -0.5, 0.5, (), jnp.float32)
    return dict(departures=departures, obs_owner=obs_owner, obs_column=obs_column, obs_count=obs_count, channel_count=channel_count, error_inv=error_inv, jacobian=jacobian, vertical=vertical)


def reference(departures, obs_owner, obs_column, obs_count, channel_count, error_inv, jacobian, vertical):
    features = NVAR * LEV
    columns_all = COLS_DEV * DEVICES
    column_index = (obs_owner[:, 0] * COLS_DEV + obs_column).astype(jnp.int32)
    row_ids = jnp.arange(NOBS_DEV * DEVICES, dtype=jnp.int32)
    block_ids = row_ids // NOBS_DEV
    live_rows = (row_ids % NOBS_DEV) < obs_count[block_ids]
    live_blocks = live_rows.reshape(DEVICES, NOBS_DEV)
    swath_blocks = jnp.arange(DEVICES, dtype=jnp.int32) % N_OBS
    channel_ids = jnp.arange(CH, dtype=jnp.int32)

    def block_adjoint(inputs):
        values, live_here, swath = inputs
        jac_swath = jacobian[swath]
        live_mask = live_here[:, None] & (channel_ids < channel_count[swath])[None, :]
        return values, jac_swath, live_mask

    def adjoint_rows_from(values_blocks, evolve):
        def one_block(inputs):
            values, jac_swath, live_mask = block_adjoint(inputs)
            if evolve:
                values = jnp.dot(values, jac_swath, preferred_element_type=jnp.float32)
            masked = jnp.where(live_mask, values, jnp.float32(0.0))
            weighted = (error_inv[inputs[2]][None, :] * masked).astype(jnp.bfloat16)
            return lax.dot_general(weighted, jac_swath, (((1,), (1,)), ((), ())), preferred_element_type=jnp.float32)
        return lax.map(one_block, (values_blocks, live_blocks, swath_blocks))

    def collect(adjoint_blocks):
        summed = jnp.zeros((columns_all, features), jnp.float32).at[column_index].add(adjoint_blocks.reshape(-1, features))
        spread = summed.T.reshape(NVAR, LEV, columns_all)
        return jnp.einsum("aij,aic->ajc", vertical, spread, precision=lax.Precision.HIGHEST)

    def system(control):
        lifted = jnp.einsum("aij,ajc->aic", vertical, control, precision=lax.Precision.HIGHEST)
        packed = lifted.reshape(features, columns_all)
        profile = packed[:, column_index].T.astype(jnp.bfloat16)
        adjoint_blocks = adjoint_rows_from(profile.reshape(DEVICES, NOBS_DEV, features), True)
        return control + collect(adjoint_blocks)

    rhs = collect(adjoint_rows_from(departures.reshape(DEVICES, NOBS_DEV, CH), False))
    increment = jnp.zeros_like(rhs)
    residual = rhs
    direction = rhs
    norm_now = jnp.sum(residual * residual)
    for iteration in range(ITERS):
        applied = system(direction)
        step_length = norm_now / jnp.sum(direction * applied)
        increment = increment + step_length * direction
        residual = residual - step_length * applied
        norm_next = jnp.sum(residual * residual)
        direction = residual + (norm_next / norm_now) * direction
        norm_now = norm_next
    return increment, residual
```

```python
import jax
import jax.numpy as jnp
from jax import lax
from jax.experimental import pallas as pl
from jax.experimental.pallas import tpu as pltpu
from jax.sharding import PartitionSpec as P

MESH = pl.DeviceIdType.MESH
BF = jnp.bfloat16
F32 = jnp.float32
COLS_DEV = 1024
NVAR, LEV = 4, 137
FEAT = NVAR * LEV
FPAD = 640
ROWS = 128
SLOTS = 256
CH = 4096
CHUNK = 512
NCHUNK = CH // CHUNK
N_COL, N_OBS = 16, 8
COL_ROWS = SLOTS // N_COL
OBS_ROWS = SLOTS // N_OBS
NT = (((1,), (1,)), ((), ()))
OBS_ORDER = (4, 5, 3, 2, 6, 7, 1)


def iota(shape, axis):
    return lax.broadcasted_iota(jnp.int32, shape, axis)


def total(value):
    return jnp.sum(jnp.sum(value, axis=0, keepdims=True), axis=1, keepdims=True)


def inner_loop(
    obs_count, channel_count, owner, column, error_inv, vertical, dep_hbm, jac_hbm,
    out_inc, out_res, out_column,
    dep, jac, lift, gram, kern, kacc, racc, sent, held, queued, rows0, prof0, hprof0, hadj0, rows1, prof1, hprof1, hadj1,
    rows2, tile_a, tile_b, in_sem, col_send, col_recv, obs_send, obs_recv, sum_send, sum_recv,
):
    col, obs = lax.axis_index("col"), lax.axis_index("obs")

    def load(chunk):
        lanes = pl.ds(pl.multiple_of(chunk * CHUNK, CHUNK), CHUNK)
        return (
            pltpu.make_async_copy(jac_hbm.at[0, :, lanes], jac.at[chunk], in_sem.at[0, chunk]),
            pltpu.make_async_copy(dep_hbm.at[:, lanes], dep.at[chunk], in_sem.at[1, chunk]),
        )

    for chunk in range(NCHUNK):
        for copy in load(chunk):
            copy.start()

    barrier = pltpu.get_barrier_semaphore()
    for step in range(1, N_OBS):
        pl.semaphore_signal(barrier, inc=1, device_id={"obs": lax.rem(obs + step, N_OBS)}, device_id_type=MESH)
    for step in range(1, N_COL):
        pl.semaphore_signal(barrier, inc=1, device_id={"col": lax.rem(col + step, N_COL)}, device_id_type=MESH)

    lift[...] = jnp.zeros_like(lift)
    for var in range(NVAR):
        lift[var * LEV : (var + 1) * LEV, var * 256 : var * 256 + LEV] = vertical[var]
    gram[...] = jnp.zeros_like(gram)
    for var in range(NVAR):
        part = lift[var * 128 : var * 128 + 256, var * 256 : var * 256 + 256]
        square = lax.dot_general(part, part, NT, precision=lax.Precision.HIGHEST, preferred_element_type=F32)
        where = slice(var * 128, var * 128 + 256)
        gram[where, where] = gram[where, where] + square

    owner_lanes = jnp.broadcast_to(owner[...].astype(F32), (ROWS, ROWS))
    owner_rows = owner_lanes.T
    earlier = jnp.where((owner_lanes == owner_rows) & (iota((ROWS, ROWS), 0) < iota((ROWS, ROWS), 1)), 1.0, 0.0)
    slot = owner[...] * 2 + jnp.sum(earlier, axis=0, keepdims=True).astype(jnp.int32)
    live_lanes = iota((1, ROWS), 1) < obs_count[0]
    place = jnp.where((iota((SLOTS, ROWS), 0) == slot) & live_lanes, 1.0, 0.0).astype(BF)
    column_rows = jnp.broadcast_to(column[...].astype(F32), (ROWS, ROWS)).T[:, 0:1]
    column_high = jnp.floor(column_rows * (1.0 / 32.0))
    column_low = column_rows - 32.0 * column_high

    def weights(chunk):
        lanes = pl.ds(pl.multiple_of(chunk * CHUNK, CHUNK), CHUNK)
        channel = chunk * CHUNK + iota((1, CHUNK), 1)
        return jnp.where(channel < channel_count[0], error_inv[:, lanes], 0.0)

    racc[...] = jnp.zeros_like(racc)

    def rhs_chunk(chunk, carry):
        for copy in load(chunk):
            copy.wait()
        weighted = (weights(chunk) * dep[chunk]).astype(BF)
        racc[:, 0:FEAT] += lax.dot_general(weighted, jac[chunk], NT, preferred_element_type=F32)
        return carry

    lax.fori_loop(0, NCHUNK, rhs_chunk, 0)
    lane = iota((ROWS, FPAD), 1)
    rows = racc[...]
    rows = jnp.where(lane == FEAT, column_high, rows)
    rows = jnp.where(lane == FEAT + 1, column_low, rows)
    rows = jnp.where(lane == FEAT + 2, 1.0, rows)
    sent[...] = jnp.dot(place, rows.astype(BF), preferred_element_type=F32).astype(BF)

    pl.semaphore_wait(barrier, N_OBS - 1 + N_COL - 1)

    def block(index, size):
        return pl.ds(pl.multiple_of(index * size, size), size)

    col_copies = []
    for step in range(1, N_COL):
        other = lax.rem(col + step, N_COL)
        copy = pltpu.make_async_remote_copy(
            src_ref=sent.at[block(other, COL_ROWS)], dst_ref=held.at[block(col, COL_ROWS)],
            send_sem=col_send.at[step], recv_sem=col_recv.at[step],
            device_id={"col": other}, device_id_type=MESH,
        )
        copy.start()
        col_copies.append(copy)
    held[block(col, COL_ROWS), :] = sent[block(col, COL_ROWS), :]

    kacc[...] = jnp.zeros_like(kacc)

    def kern_chunk(chunk, carry):
        block_in = jac[chunk]
        scaled = (block_in.astype(F32) * weights(chunk)).astype(BF)
        kacc[0:FEAT, 0:FEAT] += lax.dot_general(scaled, block_in, NT, preferred_element_type=F32)
        return carry

    lax.fori_loop(0, NCHUNK, kern_chunk, 0)
    kern[...] = kacc[...].astype(BF)

    for copy in col_copies:
        copy.wait_recv()

    target, source = iota((SLOTS, SLOTS), 0), iota((SLOTS, SLOTS), 1)
    wanted = lax.rem(target // 2, N_COL) * COL_ROWS + (target // OBS_ROWS) * 2 + lax.rem(target, 2)
    turn = jnp.where(source == wanted, 1.0, 0.0).astype(BF)
    queued[...] = jnp.dot(turn, held[...], preferred_element_type=F32).astype(BF)

    def exchange(number, source_ref, target_ref):
        copies = []
        for step in OBS_ORDER:
            other = lax.rem(obs + step, N_OBS)
            copy = pltpu.make_async_remote_copy(
                src_ref=source_ref.at[block(other, OBS_ROWS)], dst_ref=target_ref.at[block(obs, OBS_ROWS)],
                send_sem=obs_send.at[number, step], recv_sem=obs_recv.at[number, step],
                device_id={"obs": other}, device_id_type=MESH,
            )
            copy.start()
            copies.append(copy)
        target_ref[block(obs, OBS_ROWS), :] = source_ref[block(obs, OBS_ROWS), :]
        return copies

    def arrive(copies):
        for copy in copies:
            copy.wait_recv()

    first = exchange(0, queued, rows0)
    arrive(first)

    extra = rows0[:, 512:640].astype(F32)
    extra_lanes = extra.T
    at = FEAT - 512
    live = extra[:, at + 2 : at + 3]
    column_of = jnp.where(live > 0.5, extra[:, at : at + 1] * 32.0 + extra[:, at + 1 : at + 2], -1.0)
    column_across = jnp.where(
        extra_lanes[at + 2 : at + 3, :] > 0.5,
        extra_lanes[at : at + 1, :] * 32.0 + extra_lanes[at + 1 : at + 2, :],
        -2.0,
    )
    same = jnp.where(column_of == column_across, 1.0, 0.0).astype(BF)
    out_column[...] = jnp.broadcast_to(column_of, (SLOTS, 128)).astype(jnp.int32)

    gram_low = gram[...].astype(BF)

    def profile(rows_ref):
        gathered = jnp.dot(same, rows_ref[...], preferred_element_type=F32)
        return jnp.dot(gathered.astype(BF), gram_low, preferred_element_type=F32)

    def apply_kern(in_ref, out_ref):
        adjoint = jnp.dot(in_ref[...], kern[...], preferred_element_type=F32)
        out_ref[...] = adjoint.astype(BF)
        return total(adjoint * in_ref[...].astype(F32))

    lifted = profile(rows0)
    prof0[...] = lifted.astype(BF)
    second = exchange(1, prof0, hprof0)
    moment0 = total(lifted * rows0[...].astype(F32))
    arrive(second)
    moment1 = apply_kern(hprof0, hadj0)
    third = exchange(2, hadj0, rows1)
    arrive(third)
    lifted = profile(rows1)
    prof1[...] = lifted.astype(BF)
    fourth = exchange(3, prof1, hprof1)
    moment2 = total(lifted * rows1[...].astype(F32))
    arrive(fourth)
    moment3 = apply_kern(hprof1, hadj1)

    row = iota((8, 128), 0)
    mine = jnp.where(row == 0, moment0, jnp.where(row == 1, moment1, jnp.where(row == 2, moment2, jnp.where(row == 3, moment3, 0.0))))
    tile_a[obs] = mine
    sums = []
    for step in OBS_ORDER:
        copy = pltpu.make_async_remote_copy(
            src_ref=tile_a.at[obs], dst_ref=tile_a.at[obs], send_sem=sum_send.at[step], recv_sem=sum_recv.at[step],
            device_id={"obs": lax.rem(obs + step, N_OBS)}, device_id_type=MESH,
        )
        copy.start()
        sums.append(copy)
    fifth = exchange(4, hadj1, rows2)
    for copy in sums:
        copy.wait_recv()
    tile_b[col] = jnp.sum(tile_a[...], axis=0)
    sums_col = []
    for step in range(1, N_COL):
        copy = pltpu.make_async_remote_copy(
            src_ref=tile_b.at[col], dst_ref=tile_b.at[col], send_sem=sum_send.at[7 + step], recv_sem=sum_recv.at[7 + step],
            device_id={"col": lax.rem(col + step, N_COL)}, device_id_type=MESH,
        )
        copy.start()
        sums_col.append(copy)
    arrive(fifth)
    for copy in sums_col:
        copy.wait_recv()
    moments = jnp.sum(tile_b[...], axis=0)
    m0, m1, m2, m3 = (moments[index : index + 1, 0:1] for index in range(4))

    step0 = m0 / (m0 + m1)
    rest = 1.0 - step0
    norm1 = rest * rest * m0 - 2.0 * step0 * rest * m1 + step0 * step0 * m2
    dir0, dir1 = rest + norm1 / m0, -step0
    curve = dir0 * dir0 * m0 + (dir0 * (dir0 + dir1) + dir0 * dir1) * m1 + (dir0 * dir1 + dir1 * (dir0 + dir1)) * m2 + dir1 * dir1 * m3
    step1 = norm1 / curve
    q0, q1, q2 = (ref[...].astype(F32) for ref in (rows0, rows1, rows2))
    inc = (step0 + step1 * dir0) * q0 + (step1 * dir1) * q1
    res = (rest - step1 * dir0) * q0 - (step0 + step1 * (dir0 + dir1)) * q1 - (step1 * dir1) * q2
    lift_low = lift[...].astype(BF)
    out_inc[...] = jnp.dot(inc.astype(BF), lift_low, preferred_element_type=F32).astype(BF)
    out_res[...] = jnp.dot(res.astype(BF), lift_low, preferred_element_type=F32).astype(BF)

    for copies in (col_copies, first, second, third, fourth, fifth, sums, sums_col):
        for copy in copies:
            copy.wait_send()


def expand(column_of, inc, res, out_inc, out_res):
    hit = jnp.where(column_of[:, 0:1] == iota((SLOTS, COLS_DEV), 1), 1.0, 0.0).astype(BF)
    contract = (((0,), (0,)), ((), ()))
    out_inc[0] = lax.dot_general(inc[...], hit, contract, preferred_element_type=F32)[0:LEV]
    out_res[0] = lax.dot_general(res[...], hit, contract, preferred_element_type=F32)[0:LEV]


def per_device(departures, obs_owner, obs_column, obs_count, channel_count, error_inv, jacobian, vertical):
    vmem, smem = pl.BlockSpec(memory_space=pltpu.VMEM), pl.BlockSpec(memory_space=pltpu.SMEM)
    hbm = pl.BlockSpec(memory_space=pl.ANY)
    dma = pltpu.SemaphoreType.DMA
    slab = pltpu.VMEM((SLOTS, FPAD), BF)
    wide = jax.ShapeDtypeStruct((SLOTS, NVAR * 256), BF)
    inc, res, column_of = pl.pallas_call(
        inner_loop,
        out_shape=(wide, wide, jax.ShapeDtypeStruct((SLOTS, 128), jnp.int32)),
        in_specs=[smem, smem, vmem, vmem, vmem, vmem, hbm, hbm],
        out_specs=(vmem, vmem, vmem),
        scratch_shapes=[
            pltpu.VMEM((NCHUNK, ROWS, CHUNK), F32),
            pltpu.VMEM((NCHUNK, FEAT, CHUNK), BF),
            pltpu.VMEM((FPAD, NVAR * 256), F32),
            pltpu.VMEM((FPAD, FPAD), F32),
            pltpu.VMEM((FPAD, FPAD), BF),
            pltpu.VMEM((FPAD, FPAD), F32),
            pltpu.VMEM((ROWS, FPAD), F32),
            *([slab] * 12),
            pltpu.VMEM((N_OBS, 8, 128), F32),
            pltpu.VMEM((N_COL, 8, 128), F32),
            dma((2, NCHUNK)),
            dma((N_COL,)),
            dma((N_COL,)),
            dma((5, N_OBS)),
            dma((5, N_OBS)),
            dma((24,)),
            dma((24,)),
        ],
        compiler_params=pltpu.CompilerParams(collective_id=0, has_side_effects=True, vmem_limit_bytes=40 << 20),
        name="inner_loop",
    )(
        obs_count, channel_count, obs_owner.reshape(1, ROWS), obs_column.reshape(1, ROWS), error_inv, vertical, departures, jacobian
    )
    out = jax.ShapeDtypeStruct((NVAR, LEV, COLS_DEV), F32)
    return pl.pallas_call(
        expand,
        grid=(NVAR,),
        out_shape=(out, out),
        in_specs=[
            pl.BlockSpec((SLOTS, 128), lambda var: (0, 0)),
            pl.BlockSpec((SLOTS, 256), lambda var: (0, var)),
            pl.BlockSpec((SLOTS, 256), lambda var: (0, var)),
        ],
        out_specs=(
            pl.BlockSpec((1, LEV, COLS_DEV), lambda var: (var, 0, 0)),
            pl.BlockSpec((1, LEV, COLS_DEV), lambda var: (var, 0, 0)),
        ),
        compiler_params=pltpu.CompilerParams(vmem_limit_bytes=32 << 20),
        name="expand",
    )(column_of, inc, res)


def solution(mesh):
    in_specs = (
        P(("col", "obs"), None),
        P(("col", "obs"), None),
        P(("col", "obs")),
        P(("col", "obs")),
        P("obs"),
        P("obs", None),
        P("obs", None, None),
        P(),
    )
    out_specs = (P(None, None, ("col", "obs")), P(None, None, ("col", "obs")))
    return jax.shard_map(per_device, mesh=mesh, in_specs=in_specs, out_specs=out_specs, check_vma=False)
```

```python
import jax
import jax.numpy as jnp
from jax import lax
from jax.experimental import pallas as pl
from jax.experimental.pallas import tpu as pltpu
from jax.sharding import PartitionSpec as P

MESH = pl.DeviceIdType.MESH
BF = jnp.bfloat16
F32 = jnp.float32
COLS_DEV = 1024
NVAR, LEV = 4, 137
FEAT = NVAR * LEV
FPAD = 640
ROWS = 128
SLOTS = 256
CH = 4096
CHUNK = 1024
NCHUNK = CH // CHUNK
KERN_FIRST = 2
N_COL, N_OBS = 16, 8
COL_ROWS = SLOTS // N_COL
OBS_ROWS = SLOTS // N_OBS
NT = (((1,), (1,)), ((), ()))
N_CHIP = 4
CHIP_ROWS = 2 * OBS_ROWS
CHIP_ORDER = (2, 1, 3)
PLANE_ORDER = sorted(
    ((dx, dy) for dx in range(4) for dy in range(4) if dx or dy), key=lambda d: -(min(d[0], 4 - d[0]) + min(d[1], 4 - d[1]))
)


def iota(shape, axis):
    return lax.broadcasted_iota(jnp.int32, shape, axis)


def total(value):
    return jnp.sum(jnp.sum(value, axis=0, keepdims=True), axis=1, keepdims=True)


def inner_loop(
    count_hbm, channels_hbm, owner_hbm, column_hbm, error_hbm, vertical_hbm, dep_hbm, jac_hbm,
    out,
    obs_count, channel_count, owner, column, error_inv, vertical, dep, jac, lift, lift_low, gram, gram_low, kern, kacc, racc,
    same, full1, wide, split, sent, held, queued, rows0, prof0, hprof0, hadj0, rows1, prof1, hprof1, hadj1, rows2, tile_a, tile_b,
    in_sem, small_sem, col_send, col_recv, obs_send, obs_recv, sum_send, sum_recv,
):
    col, obs = lax.axis_index("col"), lax.axis_index("obs")
    chip, core = obs // 2, lax.rem(obs, 2)
    sibling = chip * 2 + 1 - core
    col_x, col_y = col // 4, lax.rem(col, 4)
    plane = [lax.rem(col_x + dx, 4) * 4 + lax.rem(col_y + dy, 4) for dx, dy in PLANE_ORDER]
    small = [
        pltpu.make_async_copy(source, target, small_sem.at[index])
        for index, (source, target) in enumerate((
            (vertical_hbm, vertical), (error_hbm, error_inv), (owner_hbm, owner), (column_hbm, column),
            (count_hbm, obs_count), (channels_hbm, channel_count),
        ))
    ]
    for copy in small:
        copy.start()

    def load(chunk):
        lanes = pl.ds(pl.multiple_of(chunk * CHUNK, CHUNK), CHUNK)
        return (
            pltpu.make_async_copy(jac_hbm.at[0, :, lanes], jac.at[chunk], in_sem.at[0, chunk]),
            pltpu.make_async_copy(dep_hbm.at[:, lanes], dep.at[chunk], in_sem.at[1, chunk]),
        )

    for chunk in range(NCHUNK):
        for copy in load(chunk):
            copy.start()

    barrier = pltpu.get_barrier_semaphore()
    for step in range(1, N_OBS):
        pl.semaphore_signal(barrier, inc=1, device_id={"obs": lax.rem(obs + step, N_OBS)}, device_id_type=MESH)
    for step in range(1, N_COL):
        pl.semaphore_signal(barrier, inc=1, device_id={"col": lax.rem(col + step, N_COL)}, device_id_type=MESH)

    for copy in small[1:]:
        copy.wait()

    owner_lanes = jnp.broadcast_to(owner[...].astype(F32), (ROWS, ROWS))
    owner_rows = owner_lanes.T
    earlier = jnp.where((owner_lanes == owner_rows) & (iota((ROWS, ROWS), 0) < iota((ROWS, ROWS), 1)), 1.0, 0.0)
    slot = owner[...] * 2 + jnp.sum(earlier, axis=0, keepdims=True).astype(jnp.int32)
    live_lanes = iota((1, ROWS), 1) < obs_count[0]
    place = jnp.where((iota((SLOTS, ROWS), 0) == slot) & live_lanes, 1.0, 0.0).astype(BF)
    column_rows = jnp.broadcast_to(column[...].astype(F32), (ROWS, ROWS)).T[:, 0:1]
    column_high = jnp.floor(column_rows * (1.0 / 32.0))
    column_low = column_rows - 32.0 * column_high

    def weights(chunk):
        lanes = pl.ds(pl.multiple_of(chunk * CHUNK, CHUNK), CHUNK)
        channel = chunk * CHUNK + iota((1, CHUNK), 1)
        return jnp.where(channel < channel_count[0], error_inv[:, lanes], 0.0)

    racc[...] = jnp.zeros_like(racc)

    def rhs_chunk(chunk, carry):
        for copy in load(chunk):
            copy.wait()
        weighted = (weights(chunk) * dep[chunk]).astype(BF)
        racc[:, 0:FEAT] += lax.dot_general(weighted, jac[chunk], NT, preferred_element_type=F32)
        return carry

    lax.fori_loop(0, NCHUNK, rhs_chunk, 0)
    lane = iota((ROWS, FPAD), 1)
    rows = racc[...]
    rows = jnp.where(lane == FEAT, column_high, rows)
    rows = jnp.where(lane == FEAT + 1, column_low, rows)
    rows = jnp.where(lane == FEAT + 2, 1.0, rows)
    sent[...] = jnp.dot(place, rows.astype(BF), preferred_element_type=F32).astype(BF)

    pl.semaphore_wait(barrier, N_OBS - 1 + N_COL - 1)

    def block(index, size):
        return pl.ds(pl.multiple_of(index * size, size), size)

    col_copies = []
    for step, other in enumerate(plane):
        copy = pltpu.make_async_remote_copy(
            src_ref=sent.at[block(other, COL_ROWS)], dst_ref=held.at[block(col, COL_ROWS)],
            send_sem=col_send.at[step], recv_sem=col_recv.at[step],
            device_id={"col": other}, device_id_type=MESH,
        )
        copy.start()
        col_copies.append(copy)
    held[block(col, COL_ROWS), :] = sent[block(col, COL_ROWS), :]

    lift[...] = jnp.zeros_like(lift)
    small[0].wait()
    for var in range(NVAR):
        lift[var * LEV : (var + 1) * LEV, var * 256 : var * 256 + LEV] = vertical[:, var, :]
    gram[...] = jnp.zeros_like(gram)
    for var in range(NVAR):
        part = lift[var * 128 : var * 128 + 256, var * 256 : var * 256 + 256]
        square = lax.dot_general(part, part, NT, precision=lax.Precision.HIGHEST, preferred_element_type=F32)
        where = slice(var * 128, var * 128 + 256)
        gram[where, where] = gram[where, where] + square

    gram_low[...] = gram[...].astype(BF)
    kacc[...] = jnp.zeros_like(kacc)

    def kern_chunk(chunk, carry):
        block_in = jac[chunk]
        scaled = (block_in.astype(F32) * weights(chunk)).astype(BF)
        kacc[0:FEAT, 0:FEAT] += lax.dot_general(scaled, block_in, NT, preferred_element_type=F32)
        return carry

    lax.fori_loop(0, KERN_FIRST, kern_chunk, 0)

    for copy in col_copies:
        copy.wait_recv()

    target, source = iota((SLOTS, SLOTS), 0), iota((SLOTS, SLOTS), 1)
    wanted = lax.rem(target // 2, N_COL) * COL_ROWS + (target // OBS_ROWS) * 2 + lax.rem(target, 2)
    turn = jnp.where(source == wanted, 1.0, 0.0).astype(BF)
    queued[...] = jnp.dot(turn, held[...], preferred_element_type=F32).astype(BF)

    sends = []

    def rows_to(number, away, source_ref, target_ref):
        there = lax.rem(chip + away, N_CHIP)
        if away == 0:
            target_ref[block(obs, OBS_ROWS), :] = source_ref[block(obs, OBS_ROWS), :]
            others = ((1, sibling),)
        else:
            others = ((0, there * 2 + core), (1, there * 2 + 1 - core))
        for which, other in others:
            copy = pltpu.make_async_remote_copy(
                src_ref=source_ref.at[block(other, OBS_ROWS)], dst_ref=target_ref.at[block(obs, OBS_ROWS)],
                send_sem=obs_send.at[number, 2 * away + which], recv_sem=obs_recv.at[number, 2 * away + which],
                device_id={"obs": other}, device_id_type=MESH,
            )
            copy.start()
            sends.append(copy)

    def rows_from(number, away, target_ref):
        there = lax.rem(chip + N_CHIP - away, N_CHIP)
        others = ((1, sibling),) if away == 0 else ((0, there * 2 + core), (1, there * 2 + 1 - core))
        for which, other in others:
            pltpu.make_async_remote_copy(
                src_ref=target_ref.at[block(other, OBS_ROWS)], dst_ref=target_ref.at[block(other, OBS_ROWS)],
                send_sem=obs_send.at[number, 2 * away + which], recv_sem=obs_recv.at[number, 2 * away + which],
                device_id={"obs": other}, device_id_type=MESH,
            ).wait_recv()
        return block(there, CHIP_ROWS)

    for away in (*CHIP_ORDER, 0):
        rows_to(0, away, queued, rows0)
    lax.fori_loop(KERN_FIRST, NCHUNK, kern_chunk, 0)
    diagonal = iota((FPAD, FPAD), 0) == iota((FPAD, FPAD), 1)
    diagonal = diagonal & (iota((FPAD, FPAD), 0) < FEAT)
    shift = (total(jnp.where(diagonal, kacc[...], 0.0)) * (1.0 / FEAT)).astype(BF).astype(F32)
    kern[...] = jnp.where(diagonal, kacc[...] - shift, kacc[...]).astype(BF)

    lane_of = iota((256, FPAD), 1)
    for var in range(NVAR):
        turned = jnp.where(lane_of == iota((256, FPAD), 0) * NVAR + var, 1.0, 0.0).astype(BF)
        part = lift[var * 128 : var * 128 + 256, var * 256 : var * 256 + 256].astype(BF)
        placed = jnp.dot(part, turned, preferred_element_type=F32).astype(BF)
        if var == 0:
            lift_low[0:256] = placed
        else:
            lift_low[var * 128 : var * 128 + 128] += placed[0:128]
            lift_low[var * 128 + 128 : var * 128 + 256] = placed[128:256]

    for away in (0, *CHIP_ORDER):
        rows_from(0, away, rows0)

    extra = rows0[:, 512:640].astype(F32)
    extra_lanes = extra.T
    at = FEAT - 512
    live = extra[:, at + 2 : at + 3]
    column_of = jnp.where(live > 0.5, extra[:, at : at + 1] * 32.0 + extra[:, at + 1 : at + 2], -1.0)
    column_across = jnp.where(
        extra_lanes[at + 2 : at + 3, :] > 0.5,
        extra_lanes[at : at + 1, :] * 32.0 + extra_lanes[at + 1 : at + 2, :],
        -2.0,
    )
    same[...] = jnp.where(column_of == column_across, 1.0, 0.0).astype(BF)

    def halves(value):
        high = value.astype(BF)
        return high, (value - high.astype(F32)).astype(BF)

    def send_profiles(number, gathered, prof_ref, target_ref, own):
        high, low = halves(gathered)
        split[0] = high
        split[1] = low
        moment = jnp.zeros((1, 1), F32)
        for away in (*CHIP_ORDER, 0):
            here = block(lax.rem(chip + away, N_CHIP), CHIP_ROWS)
            pair = jnp.concatenate([split[0, here, :], split[1, here, :]], axis=0)
            both = jnp.dot(pair, gram_low[...], preferred_element_type=F32)
            lifted = both[0:CHIP_ROWS] + both[CHIP_ROWS:]
            prof_ref[here, :] = lifted.astype(BF)
            rows_to(number, away, prof_ref, target_ref)
            moment += total(lifted * own[here, :].astype(F32))
        return moment

    def apply_kern(number, prof_ref, adj_ref, target_ref, after):
        moment = jnp.zeros((1, 1), F32)
        lane_here = iota((CHIP_ROWS, FPAD), 1)
        for away in (0, 1, 3, 2):
            here = rows_from(number, away, prof_ref)
            profiles = prof_ref[here, :]
            adjoint = jnp.dot(profiles, kern[...], preferred_element_type=F32)
            adj_ref[here, :] = jnp.where(lane_here == FEAT, shift, adjoint).astype(BF)
            profiles = profiles.astype(F32)
            if after is None:
                rows_to(number + 1, (N_CHIP - away) % N_CHIP, adj_ref, target_ref)
            moment += total(profiles * (adjoint + shift * profiles))
            if after is not None:
                if away == 2:
                    after(moment)
                rows_to(number + 1, (N_CHIP - away) % N_CHIP, adj_ref, target_ref)
        return moment

    def whole(adj_ref, prof_ref):
        adjoint = adj_ref[...].astype(F32)
        shifts = adjoint[:, FEAT : FEAT + 1]
        return jnp.where(iota((SLOTS, FPAD), 1) < FEAT, adjoint + shifts * prof_ref[...].astype(F32), 0.0)

    gathered = jnp.dot(same[...], rows0[...], preferred_element_type=F32)
    moment0 = send_profiles(1, gathered, prof0, hprof0, rows0)
    moment1 = apply_kern(1, hprof0, hadj0, rows1, None)
    for away in (0, *CHIP_ORDER):
        rows_from(2, away, rows1)
    full1[...] = whole(rows1, prof0)
    high, low = halves(full1[...])
    gathered = jnp.dot(same[...], high, preferred_element_type=F32) + jnp.dot(same[...], low, preferred_element_type=F32)
    moment2 = send_profiles(3, gathered, prof1, hprof1, full1)

    row = iota((8, 128), 0)
    sums = []

    def send_moments(moment3):
        tile_a[obs] = jnp.where(
            row == 0, moment0, jnp.where(row == 1, moment1, jnp.where(row == 2, moment2, jnp.where(row == 3, moment3, 0.0)))
        )
        for step in (4, 5, 3, 2, 6, 7, 1):
            copy = pltpu.make_async_remote_copy(
                src_ref=tile_a.at[obs], dst_ref=tile_a.at[obs], send_sem=sum_send.at[step], recv_sem=sum_recv.at[step],
                device_id={"obs": lax.rem(obs + step, N_OBS)}, device_id_type=MESH,
            )
            copy.start()
            sums.append(copy)

    apply_kern(3, hprof1, hadj1, rows2, send_moments)
    for copy in sums:
        copy.wait_recv()
    tile_b[col] = jnp.sum(tile_a[...], axis=0)
    sums_col = []
    for step, other in enumerate(plane):
        copy = pltpu.make_async_remote_copy(
            src_ref=tile_b.at[col], dst_ref=tile_b.at[col], send_sem=sum_send.at[8 + step], recv_sem=sum_recv.at[8 + step],
            device_id={"col": other}, device_id_type=MESH,
        )
        copy.start()
        sums_col.append(copy)
    for away in (0, *CHIP_ORDER):
        rows_from(4, away, rows2)
    wide[0] = jnp.dot(rows0[...], lift_low[...], preferred_element_type=F32)
    high, low = halves(full1[...])
    wide[1] = jnp.dot(high, lift_low[...], preferred_element_type=F32) + jnp.dot(low, lift_low[...], preferred_element_type=F32)
    high, low = halves(whole(rows2, prof1))
    wide[2] = jnp.dot(high, lift_low[...], preferred_element_type=F32) + jnp.dot(low, lift_low[...], preferred_element_type=F32)
    for copy in sums_col:
        copy.wait_recv()
    moments = jnp.sum(tile_b[...], axis=0)
    m0, m1, m2, m3 = (moments[index : index + 1, 0:1] for index in range(4))

    step0 = m0 / (m0 + m1)
    rest = 1.0 - step0
    norm1 = rest * rest * m0 - 2.0 * step0 * rest * m1 + step0 * step0 * m2
    dir0, dir1 = rest + norm1 / m0, -step0
    curve = dir0 * dir0 * m0 + (dir0 * (dir0 + dir1) + dir0 * dir1) * m1 + (dir0 * dir1 + dir1 * (dir0 + dir1)) * m2 + dir1 * dir1 * m3
    step1 = norm1 / curve
    tail = iota((SLOTS, FPAD), 1) >= FEAT
    inc = (step0 + step1 * dir0) * wide[0] + (step1 * dir1) * wide[1]
    res = (rest - step1 * dir0) * wide[0] - (step0 + step1 * (dir0 + dir1)) * wide[1] - (step1 * dir1) * wide[2]
    out[0] = jnp.where(tail, rows0[...].astype(F32), inc).astype(BF)
    out[1] = jnp.where(tail, 0.0, res).astype(BF)

    for copy in (*col_copies, *sends, *sums, *sums_col):
        copy.wait_send()


def expand(packed, out_inc, out_res, taken, full_inc, full_res, in_sem, out_sem):
    parts = FPAD // 128
    levels = 128 // NVAR
    order = (parts - 1, *range(parts - 1))
    loads = [
        pltpu.make_async_copy(packed.at[:, :, pl.ds(128 * part, 128)], taken.at[part], in_sem.at[part]) for part in range(parts)
    ]
    for part in order:
        loads[part].start()
    loads[parts - 1].wait()
    extra = taken[parts - 1, 0].astype(F32)
    at = FEAT - 512
    column_of = jnp.where(extra[:, at + 2 : at + 3] > 0.5, extra[:, at : at + 1] * 32.0 + extra[:, at + 1 : at + 2], -1.0)
    hit = jnp.where(column_of.astype(jnp.int32) == iota((SLOTS, COLS_DEV), 1), 1.0, 0.0).astype(BF)
    contract = (((0,), (0,)), ((), ()))
    stores = []
    for part in order:
        if part < parts - 1:
            loads[part].wait()
        count = min(levels, LEV - levels * part)
        for index, (full, out) in enumerate(((full_inc, out_inc), (full_res, out_res))):
            values = lax.dot_general(taken[part, index], hit, contract, preferred_element_type=F32)
            full[levels * part : levels * part + count] = values[0 : NVAR * count].reshape(count, NVAR, COLS_DEV)
            here = pl.ds(levels * part, count)
            store = pltpu.make_async_copy(full.at[here], out.at[here], out_sem.at[part, index])
            store.start()
            stores.append(store)
    for store in stores:
        store.wait()


def per_device(departures, obs_owner, obs_column, obs_count, channel_count, error_inv, jacobian, vertical):
    vmem, hbm = pl.BlockSpec(memory_space=pltpu.VMEM), pl.BlockSpec(memory_space=pltpu.HBM)
    dma = pltpu.SemaphoreType.DMA
    slab = pltpu.VMEM((SLOTS, FPAD), BF)
    packed = pl.pallas_call(
        inner_loop,
        out_shape=jax.ShapeDtypeStruct((2, SLOTS, FPAD), BF),
        in_specs=[hbm] * 8,
        out_specs=vmem,
        scratch_shapes=[
            pltpu.SMEM((1,), jnp.int32),
            pltpu.SMEM((1,), jnp.int32),
            pltpu.VMEM((1, ROWS), jnp.int32),
            pltpu.VMEM((1, ROWS), jnp.int32),
            pltpu.VMEM((1, CH), F32),
            pltpu.VMEM((LEV, NVAR, LEV), F32),
            pltpu.VMEM((NCHUNK, ROWS, CHUNK), F32),
            pltpu.VMEM((NCHUNK, FEAT, CHUNK), BF),
            pltpu.VMEM((FPAD, NVAR * 256), F32),
            pltpu.VMEM((FPAD, FPAD), BF),
            pltpu.VMEM((FPAD, FPAD), F32),
            pltpu.VMEM((FPAD, FPAD), BF),
            pltpu.VMEM((FPAD, FPAD), BF),
            pltpu.VMEM((FPAD, FPAD), F32),
            pltpu.VMEM((ROWS, FPAD), F32),
            pltpu.VMEM((SLOTS, SLOTS), BF),
            pltpu.VMEM((SLOTS, FPAD), F32),
            pltpu.VMEM((3, SLOTS, FPAD), F32),
            pltpu.VMEM((2, SLOTS, FPAD), BF),
            *([slab] * 12),
            pltpu.VMEM((N_OBS, 8, 128), F32),
            pltpu.VMEM((N_COL, 8, 128), F32),
            dma((2, NCHUNK)),
            dma((6,)),
            dma((N_COL,)),
            dma((N_COL,)),
            dma((5, N_OBS)),
            dma((5, N_OBS)),
            dma((24,)),
            dma((24,)),
        ],
        compiler_params=pltpu.CompilerParams(collective_id=0, has_side_effects=True, vmem_limit_bytes=62 << 20),
        name="inner_loop",
    )(
        obs_count, channel_count, obs_owner.reshape(1, ROWS), obs_column.reshape(1, ROWS), error_inv,
        vertical.transpose(1, 0, 2), departures, jacobian,
    )
    out = jax.ShapeDtypeStruct((LEV, NVAR, COLS_DEV), F32)
    inc, res = pl.pallas_call(
        expand,
        out_shape=(out, out),
        in_specs=[hbm],
        out_specs=(hbm, hbm),
        scratch_shapes=[
            pltpu.VMEM((FPAD // 128, 2, SLOTS, 128), BF),
            pltpu.VMEM((LEV, NVAR, COLS_DEV), F32),
            pltpu.VMEM((LEV, NVAR, COLS_DEV), F32),
            dma((FPAD // 128,)),
            dma((FPAD // 128, 2)),
        ],
        compiler_params=pltpu.CompilerParams(vmem_limit_bytes=62 << 20),
        name="expand",
    )(packed)
    return inc.transpose(1, 0, 2), res.transpose(1, 0, 2)


def solution(mesh):
    in_specs = (
        P(("col", "obs"), None),
        P(("col", "obs"), None),
        P(("col", "obs")),
        P(("col", "obs")),
        P("obs"),
        P("obs", None),
        P("obs", None, None),
        P(),
    )
    out_specs = (P(None, None, ("col", "obs")), P(None, None, ("col", "obs")))
    return jax.shard_map(per_device, mesh=mesh, in_specs=in_specs, out_specs=out_specs, check_vma=False)
```

```python
import jax
import jax.numpy as jnp
from jax import lax
from jax.experimental import pallas as pl
from jax.experimental.pallas import tpu as pltpu
from jax.sharding import PartitionSpec as P

MESH = pl.DeviceIdType.MESH
BF = jnp.bfloat16
F32 = jnp.float32
COLS_DEV = 1024
NVAR, LEV = 4, 137
FEAT = NVAR * LEV
FPAD = 640
ROWS = 128
SLOTS = 256
CH = 4096
CHUNK = 1024
NCHUNK = CH // CHUNK
K_PARTS = ((0, 560, 0), (128, 432, 128), (640, 304, 0), (768, 176, 128), (1024, 48, 0))
K_FREE = ((560, 80), (944, 80), (1072, 80))
K_ROWS = 1152
GUESTS = 5
N_COL, N_OBS = 16, 8
COL_ROWS = SLOTS // N_COL
OBS_ROWS = SLOTS // N_OBS
NT = (((1,), (1,)), ((), ()))
N_CHIP = 4
CHIP_ROWS = 2 * OBS_ROWS
CHIP_ORDER = (2, 1, 3)
PLANE_ORDER = sorted(
    ((dx, dy) for dx in range(4) for dy in range(4) if dx or dy), key=lambda d: -(min(d[0], 4 - d[0]) + min(d[1], 4 - d[1]))
)


def iota(shape, axis):
    return lax.broadcasted_iota(jnp.int32, shape, axis)


def total(value):
    return jnp.sum(jnp.sum(value, axis=0, keepdims=True), axis=1, keepdims=True)


def inner_loop(
    count_hbm, channels_hbm, owner_hbm, column_hbm, error_hbm, vertical_hbm, dep_hbm, jac_hbm,
    out,
    obs_count, channel_count, owner, column, error_inv, vertical, dep, jac, lift, lift_low, gram, gram_low, kern, kacc, racc,
    same, full1, wide, split, sent, held, queued, rows0, prof0, rows1, prof1, rows2, guest0, reply0, guest1, reply1, tile_a, tile_b,
    in_sem, small_sem, col_send, col_recv, obs_send, obs_recv, kern_send, kern_recv, leg_send, leg_recv, sum_send, sum_recv,
):
    col, obs = lax.axis_index("col"), lax.axis_index("obs")
    chip, core = obs // 2, lax.rem(obs, 2)
    sibling = chip * 2 + 1 - core
    col_x, col_y = col // 4, lax.rem(col, 4)
    plane = [lax.rem(col_x + dx, 4) * 4 + lax.rem(col_y + dy, 4) for dx, dy in PLANE_ORDER]
    small = [
        pltpu.make_async_copy(source, target, small_sem.at[index])
        for index, (source, target) in enumerate((
            (vertical_hbm, vertical), (error_hbm, error_inv), (owner_hbm, owner), (column_hbm, column),
            (count_hbm, obs_count), (channels_hbm, channel_count),
        ))
    ]
    for copy in small:
        copy.start()

    def load(chunk):
        lanes = pl.ds(pl.multiple_of(chunk * CHUNK, CHUNK), CHUNK)
        return (
            pltpu.make_async_copy(jac_hbm.at[0, :, lanes], jac.at[chunk], in_sem.at[0, chunk]),
            pltpu.make_async_copy(dep_hbm.at[:, lanes], dep.at[chunk], in_sem.at[1, chunk]),
        )

    for chunk in range(NCHUNK):
        for copy in load(chunk):
            copy.start()

    barrier = pltpu.get_barrier_semaphore()
    for step in range(1, N_OBS):
        pl.semaphore_signal(barrier, inc=1, device_id={"obs": lax.rem(obs + step, N_OBS)}, device_id_type=MESH)
    for step in range(1, N_COL):
        pl.semaphore_signal(barrier, inc=1, device_id={"col": lax.rem(col + step, N_COL)}, device_id_type=MESH)

    for copy in small[1:]:
        copy.wait()

    owner_lanes = jnp.broadcast_to(owner[...].astype(F32), (ROWS, ROWS))
    owner_rows = owner_lanes.T
    earlier = jnp.where((owner_lanes == owner_rows) & (iota((ROWS, ROWS), 0) < iota((ROWS, ROWS), 1)), 1.0, 0.0)
    slot = owner[...] * 2 + jnp.sum(earlier, axis=0, keepdims=True).astype(jnp.int32)
    live_lanes = iota((1, ROWS), 1) < obs_count[0]
    place = jnp.where((iota((SLOTS, ROWS), 0) == slot) & live_lanes, 1.0, 0.0).astype(BF)
    column_rows = jnp.broadcast_to(column[...].astype(F32), (ROWS, ROWS)).T[:, 0:1]
    column_high = jnp.floor(column_rows * (1.0 / 32.0))
    column_low = column_rows - 32.0 * column_high

    def weights(chunk):
        lanes = pl.ds(pl.multiple_of(chunk * CHUNK, CHUNK), CHUNK)
        channel = chunk * CHUNK + iota((1, CHUNK), 1)
        return jnp.where(channel < channel_count[0], error_inv[:, lanes], 0.0)

    racc[...] = jnp.zeros_like(racc)

    def rhs_chunk(chunk, carry):
        for copy in load(chunk):
            copy.wait()
        weighted = (weights(chunk) * dep[chunk]).astype(BF)
        racc[:, 0:FEAT] += lax.dot_general(weighted, jac[chunk], NT, preferred_element_type=F32)
        return carry

    lax.fori_loop(0, NCHUNK, rhs_chunk, 0)
    lane = iota((ROWS, FPAD), 1)
    rows = racc[...]
    rows = jnp.where(lane == FEAT, column_high, rows)
    rows = jnp.where(lane == FEAT + 1, column_low, rows)
    rows = jnp.where(lane == FEAT + 2, 1.0, rows)
    sent[...] = jnp.dot(place, rows.astype(BF), preferred_element_type=F32).astype(BF)

    pl.semaphore_wait(barrier, N_OBS - 1 + N_COL - 1)

    def block(index, size):
        return pl.ds(pl.multiple_of(index * size, size), size)

    col_copies = []
    for step, other in enumerate(plane):
        copy = pltpu.make_async_remote_copy(
            src_ref=sent.at[block(other, COL_ROWS)], dst_ref=held.at[block(col, COL_ROWS)],
            send_sem=col_send.at[step], recv_sem=col_recv.at[step],
            device_id={"col": other}, device_id_type=MESH,
        )
        copy.start()
        col_copies.append(copy)
    held[block(col, COL_ROWS), :] = sent[block(col, COL_ROWS), :]

    for first, count in K_FREE:
        kern[:, first : first + count, :] = jnp.zeros((3, count, 256), BF)
    kern_copies = []
    diagonal = iota((128, 128), 0) == iota((128, 128), 1)

    def kern_part(which, index):
        first, count, lane_at = K_PARTS[index]
        return kern.at[which, pl.ds(first, count), pl.ds(lane_at, 128)]

    def make_kern(index, shift):
        first, count, lane_at = K_PARTS[index]
        lanes = slice(lane_at, lane_at + 128)
        top = index * 128
        wide_rows = min(128, FEAT - top)
        kacc[...] = jnp.zeros_like(kacc)

        def kern_chunk(chunk, carry):
            scaled = (jac[chunk, top : top + wide_rows, :].astype(F32) * weights(chunk)).astype(BF)
            kacc[0 : FEAT - top, 0:wide_rows] += lax.dot_general(
                jac[chunk, top:FEAT, :], scaled, NT, preferred_element_type=F32
            )
            return carry

        lax.fori_loop(0, NCHUNK, kern_chunk, 0)
        if index == 0:
            shift = (total(jnp.where(diagonal, kacc[0:128], 0.0)) * (1.0 / 128)).astype(BF).astype(F32)
        if wide_rows < 128:
            corner = jnp.where(diagonal, kacc[0:128] - shift, kacc[0:128])
            kern[1, first : first + count, lanes] = jnp.where(iota((128, 128), 0) < wide_rows, corner, shift)[0:count].astype(BF)
        else:
            kern[1, first : first + 128, lanes] = jnp.where(diagonal, kacc[0:128] - shift, kacc[0:128]).astype(BF)
            kern[1, first + 128 : first + count, lanes] = kacc[128:count].astype(BF)
        for target, away in ((0, 1), (2, 3)):
            copy = pltpu.make_async_remote_copy(
                src_ref=kern_part(1, index), dst_ref=kern_part(target, index),
                send_sem=kern_send.at[target, index], recv_sem=kern_recv.at[target, index],
                device_id={"obs": lax.rem(chip + away, N_CHIP) * 2 + core}, device_id_type=MESH,
            )
            copy.start()
            kern_copies.append(copy)
        return shift

    def fill_kern(which):
        for first in (0, 640):
            kern[which, first : first + 128, 128:256] = kern[which, first + 128 : first + 256, 0:128].astype(F32).T.astype(BF)

    shift = make_kern(0, None)
    make_kern(1, shift)

    for copy in col_copies:
        copy.wait_recv()

    target, source = iota((SLOTS, SLOTS), 0), iota((SLOTS, SLOTS), 1)
    wanted = lax.rem(target // 2, N_COL) * COL_ROWS + (target // OBS_ROWS) * 2 + lax.rem(target, 2)
    turn = jnp.where(source == wanted, 1.0, 0.0).astype(BF)
    queued[...] = jnp.dot(turn, held[...], preferred_element_type=F32).astype(BF)

    sends = []

    def rows_to(number, away, source_ref, target_ref):
        there = lax.rem(chip + away, N_CHIP)
        if away == 0:
            target_ref[block(obs, OBS_ROWS), :] = source_ref[block(obs, OBS_ROWS), :]
            others = ((1, sibling),)
        else:
            others = ((0, there * 2 + core), (1, there * 2 + 1 - core))
        for which, other in others:
            copy = pltpu.make_async_remote_copy(
                src_ref=source_ref.at[block(other, OBS_ROWS)], dst_ref=target_ref.at[block(obs, OBS_ROWS)],
                send_sem=obs_send.at[number, 2 * away + which], recv_sem=obs_recv.at[number, 2 * away + which],
                device_id={"obs": other}, device_id_type=MESH,
            )
            copy.start()
            sends.append(copy)

    def rows_from(number, away, target_ref):
        there = lax.rem(chip + N_CHIP - away, N_CHIP)
        others = ((1, sibling),) if away == 0 else ((0, there * 2 + core), (1, there * 2 + 1 - core))
        for which, other in others:
            pltpu.make_async_remote_copy(
                src_ref=target_ref.at[block(other, OBS_ROWS)], dst_ref=target_ref.at[block(other, OBS_ROWS)],
                send_sem=obs_send.at[number, 2 * away + which], recv_sem=obs_recv.at[number, 2 * away + which],
                device_id={"obs": other}, device_id_type=MESH,
            ).wait_recv()
        return block(there, CHIP_ROWS)

    for away in (*CHIP_ORDER, 0):
        rows_to(0, away, queued, rows0)
    for index in (2, 3, 4):
        make_kern(index, shift)
    fill_kern(1)
    lift[...] = jnp.zeros_like(lift)
    small[0].wait()
    for var in range(NVAR):
        lift[var * LEV : (var + 1) * LEV, var * 256 : var * 256 + LEV] = vertical[:, var, :]
    gram[...] = jnp.zeros_like(gram)
    for var in range(NVAR):
        part = lift[var * 128 : var * 128 + 256, var * 256 : var * 256 + 256]
        square = lax.dot_general(part, part, NT, precision=lax.Precision.HIGHEST, preferred_element_type=F32)
        where = slice(var * 128, var * 128 + 256)
        gram[where, where] = gram[where, where] + square

    gram_low[...] = gram[...].astype(BF)
    lane_of = iota((256, FPAD), 1)
    for var in range(NVAR):
        turned = jnp.where(lane_of == iota((256, FPAD), 0) * NVAR + var, 1.0, 0.0).astype(BF)
        part = lift[var * 128 : var * 128 + 256, var * 256 : var * 256 + 256].astype(BF)
        placed = jnp.dot(part, turned, preferred_element_type=F32).astype(BF)
        if var == 0:
            lift_low[0:256] = placed
        else:
            lift_low[var * 128 : var * 128 + 128] += placed[0:128]
            lift_low[var * 128 + 128 : var * 128 + 256] = placed[128:256]

    for away in (0, *CHIP_ORDER):
        rows_from(0, away, rows0)

    extra = rows0[:, 512:640].astype(F32)
    extra_lanes = extra.T
    at = FEAT - 512
    live = extra[:, at + 2 : at + 3]
    column_of = jnp.where(live > 0.5, extra[:, at : at + 1] * 32.0 + extra[:, at + 1 : at + 2], -1.0)
    column_across = jnp.where(
        extra_lanes[at + 2 : at + 3, :] > 0.5,
        extra_lanes[at : at + 1, :] * 32.0 + extra_lanes[at + 1 : at + 2, :],
        -2.0,
    )
    same[...] = jnp.where(column_of == column_across, 1.0, 0.0).astype(BF)

    def halves(value):
        high = value.astype(BF)
        return high, (value - high.astype(F32)).astype(BF)

    def send_profiles(number, gathered, prof_ref, target_ref, own):
        high, low = halves(gathered)
        split[0] = high
        split[1] = low
        moment = jnp.zeros((1, 1), F32)
        for away in (*CHIP_ORDER, 0):
            here = block(lax.rem(chip + away, N_CHIP), CHIP_ROWS)
            pair = jnp.concatenate([split[0, here, :], split[1, here, :]], axis=0)
            both = jnp.dot(pair, gram_low[...], preferred_element_type=F32)
            lifted = both[0:CHIP_ROWS] + both[CHIP_ROWS:]
            prof_ref[here, :] = lifted.astype(BF)
            profiles_to(number, away, prof_ref, target_ref)
            moment += total(lifted * own[here, :].astype(F32))
        return moment

    def slab(chip_index, core_index):
        return block(lax.rem(chip_index, N_CHIP) * 2 + core_index, OBS_ROWS)

    def copy_of(number, source, target, send, recv, device):
        return pltpu.make_async_remote_copy(
            src_ref=source, dst_ref=target, send_sem=leg_send.at[number, send], recv_sem=leg_recv.at[number, recv],
            device_id={"obs": device}, device_id_type=MESH,
        )

    helper = lax.rem(chip + 1 + 2 * core, N_CHIP)

    def go(copy):
        copy.start()
        sends.append(copy)

    def profiles_to(number, away, prof_ref, guest_ref):
        if away == 2:
            for other in range(2):
                go(copy_of(number, prof_ref.at[slab(chip + 2, other)], guest_ref.at[4 - core], 3 + other, 4 - core, helper * 2 + other))
        else:
            slot = (away + 1) % N_CHIP
            go(copy_of(number, prof_ref.at[slab(chip + away, 1 - core)], guest_ref.at[slot], slot, slot, sibling))

    def apply_kern(number, prof_ref, guest_ref, reply_ref, target_ref, after):
        moment = jnp.zeros((1, 1), F32)
        for which, guests in ((1, (1,)), (0, (3, 0)), (2, (4, 2))):
            own = slab(chip + which + 3, core)
            for guest in guests:
                copy_of(number, guest_ref.at[guest], guest_ref.at[guest], guest, guest, sibling).wait_recv()
            if number == 0 and which != 1:
                for index in range(len(K_PARTS)):
                    part = kern_part(which, index)
                    pltpu.make_async_remote_copy(
                        src_ref=part, dst_ref=part, send_sem=kern_send.at[which, index], recv_sem=kern_recv.at[which, index],
                        device_id={"obs": sibling}, device_id_type=MESH,
                    ).wait_recv()
                fill_kern(which)
            profiles = jnp.concatenate([prof_ref[own, :]] + [guest_ref[guest] for guest in guests], axis=0)
            left, middle, right = profiles[:, 0:256], profiles[:, 256:512], profiles[:, 512:640]
            dot = lambda one, two: jnp.dot(one, two, preferred_element_type=F32)
            dot_turned = lambda one, two: lax.dot_general(one, two, NT, preferred_element_type=F32)
            adjoint = jnp.concatenate(
                [
                    dot(profiles, kern[which, 0:640, :]),
                    dot_turned(left, kern[which, 256:512, :]) + dot(profiles[:, 256:640], kern[which, 640:1024, :]),
                    dot_turned(left, kern[which, 512:640, :]) + dot_turned(middle, kern[which, 896:1024, :])
                    + dot(right, kern[which, 1024:1152, 0:128]),
                ],
                axis=1,
            )
            away_shift = kern[which, 1056:1072, 0:128].astype(F32)[8:9, 0:1]
            rows_out = jnp.where(iota(adjoint.shape, 1) == FEAT, away_shift, adjoint).astype(BF)
            profiles = profiles.astype(F32)
            moment += total(profiles * (adjoint + away_shift * profiles))
            target_ref[own, :] = rows_out[0:OBS_ROWS]
            for index, guest in enumerate(guests):
                reply_ref[guest] = rows_out[(index + 1) * OBS_ROWS : (index + 2) * OBS_ROWS]
            if after is not None and which == 2:
                after(moment)
            for guest in guests:
                if guest < 3:
                    go(copy_of(number + 1, reply_ref.at[guest], target_ref.at[own], guest, guest, sibling))
                else:
                    back = lax.rem(chip + (1 if guest == 3 else 3), N_CHIP) * 2 + (1 if guest == 3 else 0)
                    go(copy_of(number + 1, reply_ref.at[guest], target_ref.at[own], guest, 3 + core, back))
        return moment

    def replies(number, target_ref):
        for slot in range(3):
            here = target_ref.at[slab(chip + slot + 3, 1 - core)]
            copy_of(number, here, here, slot, slot, sibling).wait_recv()
        for other in range(2):
            here = target_ref.at[slab(chip + 2, other)]
            copy_of(number, here, here, 3 + other, 3 + other, sibling).wait_recv()

    def whole(adj_ref, prof_ref):
        adjoint = adj_ref[...].astype(F32)
        shifts = adjoint[:, FEAT : FEAT + 1]
        return jnp.where(iota((SLOTS, FPAD), 1) < FEAT, adjoint + shifts * prof_ref[...].astype(F32), 0.0)

    gathered = jnp.dot(same[...], rows0[...], preferred_element_type=F32)
    moment0 = send_profiles(0, gathered, prof0, guest0, rows0)
    moment1 = apply_kern(0, prof0, guest0, reply0, rows1, None)
    replies(1, rows1)
    full1[...] = whole(rows1, prof0)
    high, low = halves(full1[...])
    gathered = jnp.dot(same[...], high, preferred_element_type=F32) + jnp.dot(same[...], low, preferred_element_type=F32)
    moment2 = send_profiles(2, gathered, prof1, guest1, full1)

    row = iota((8, 128), 0)
    sums = []

    def send_moments(moment3):
        tile_a[obs] = jnp.where(
            row == 0, moment0, jnp.where(row == 1, moment1, jnp.where(row == 2, moment2, jnp.where(row == 3, moment3, 0.0)))
        )
        for step in (4, 5, 3, 2, 6, 7, 1):
            copy = pltpu.make_async_remote_copy(
                src_ref=tile_a.at[obs], dst_ref=tile_a.at[obs], send_sem=sum_send.at[step], recv_sem=sum_recv.at[step],
                device_id={"obs": lax.rem(obs + step, N_OBS)}, device_id_type=MESH,
            )
            copy.start()
            sums.append(copy)

    apply_kern(2, prof1, guest1, reply1, rows2, send_moments)
    for copy in sums:
        copy.wait_recv()
    tile_b[col] = jnp.sum(tile_a[...], axis=0)
    sums_col = []
    for step, other in enumerate(plane):
        copy = pltpu.make_async_remote_copy(
            src_ref=tile_b.at[col], dst_ref=tile_b.at[col], send_sem=sum_send.at[8 + step], recv_sem=sum_recv.at[8 + step],
            device_id={"col": other}, device_id_type=MESH,
        )
        copy.start()
        sums_col.append(copy)
    replies(3, rows2)
    wide[0] = jnp.dot(rows0[...], lift_low[...], preferred_element_type=F32)
    high, low = halves(full1[...])
    wide[1] = jnp.dot(high, lift_low[...], preferred_element_type=F32) + jnp.dot(low, lift_low[...], preferred_element_type=F32)
    high, low = halves(whole(rows2, prof1))
    wide[2] = jnp.dot(high, lift_low[...], preferred_element_type=F32) + jnp.dot(low, lift_low[...], preferred_element_type=F32)
    for copy in sums_col:
        copy.wait_recv()
    moments = jnp.sum(tile_b[...], axis=0)
    m0, m1, m2, m3 = (moments[index : index + 1, 0:1] for index in range(4))

    step0 = m0 / (m0 + m1)
    rest = 1.0 - step0
    norm1 = rest * rest * m0 - 2.0 * step0 * rest * m1 + step0 * step0 * m2
    dir0, dir1 = rest + norm1 / m0, -step0
    curve = dir0 * dir0 * m0 + (dir0 * (dir0 + dir1) + dir0 * dir1) * m1 + (dir0 * dir1 + dir1 * (dir0 + dir1)) * m2 + dir1 * dir1 * m3
    step1 = norm1 / curve
    tail = iota((SLOTS, FPAD), 1) >= FEAT
    inc = (step0 + step1 * dir0) * wide[0] + (step1 * dir1) * wide[1]
    res = (rest - step1 * dir0) * wide[0] - (step0 + step1 * (dir0 + dir1)) * wide[1] - (step1 * dir1) * wide[2]
    out[0] = jnp.where(tail, rows0[...].astype(F32), inc).astype(BF)
    out[1] = jnp.where(tail, 0.0, res).astype(BF)

    for copy in (*col_copies, *kern_copies, *sends, *sums, *sums_col):
        copy.wait_send()


def expand(packed, out_inc, out_res, taken, full_inc, full_res, in_sem, out_sem):
    parts = FPAD // 128
    levels = 128 // NVAR
    order = (parts - 1, *range(parts - 1))
    loads = [
        pltpu.make_async_copy(packed.at[:, :, pl.ds(128 * part, 128)], taken.at[part], in_sem.at[part]) for part in range(parts)
    ]
    for part in order:
        loads[part].start()
    loads[parts - 1].wait()
    extra = taken[parts - 1, 0].astype(F32)
    at = FEAT - 512
    column_of = jnp.where(extra[:, at + 2 : at + 3] > 0.5, extra[:, at : at + 1] * 32.0 + extra[:, at + 1 : at + 2], -1.0)
    hit = jnp.where(column_of.astype(jnp.int32) == iota((SLOTS, COLS_DEV), 1), 1.0, 0.0).astype(BF)
    contract = (((0,), (0,)), ((), ()))
    stores = []
    for part in order:
        if part < parts - 1:
            loads[part].wait()
        count = min(levels, LEV - levels * part)
        for index, (full, out) in enumerate(((full_inc, out_inc), (full_res, out_res))):
            values = lax.dot_general(taken[part, index], hit, contract, preferred_element_type=F32)
            full[levels * part : levels * part + count] = values[0 : NVAR * count].reshape(count, NVAR, COLS_DEV)
            here = pl.ds(levels * part, count)
            store = pltpu.make_async_copy(full.at[here], out.at[here], out_sem.at[part, index])
            store.start()
            stores.append(store)
    for store in stores:
        store.wait()


def per_device(departures, obs_owner, obs_column, obs_count, channel_count, error_inv, jacobian, vertical):
    vmem, hbm = pl.BlockSpec(memory_space=pltpu.VMEM), pl.BlockSpec(memory_space=pltpu.HBM)
    dma = pltpu.SemaphoreType.DMA
    slab = pltpu.VMEM((SLOTS, FPAD), BF)
    packed = pl.pallas_call(
        inner_loop,
        out_shape=jax.ShapeDtypeStruct((2, SLOTS, FPAD), BF),
        in_specs=[hbm] * 8,
        out_specs=vmem,
        scratch_shapes=[
            pltpu.SMEM((1,), jnp.int32),
            pltpu.SMEM((1,), jnp.int32),
            pltpu.VMEM((1, ROWS), jnp.int32),
            pltpu.VMEM((1, ROWS), jnp.int32),
            pltpu.VMEM((1, CH), F32),
            pltpu.VMEM((LEV, NVAR, LEV), F32),
            pltpu.VMEM((NCHUNK, ROWS, CHUNK), F32),
            pltpu.VMEM((NCHUNK, FEAT, CHUNK), BF),
            pltpu.VMEM((FPAD, NVAR * 256), F32),
            pltpu.VMEM((FPAD, FPAD), BF),
            pltpu.VMEM((FPAD, FPAD), F32),
            pltpu.VMEM((FPAD, FPAD), BF),
            pltpu.VMEM((3, K_ROWS, 256), BF),
            pltpu.VMEM((FPAD, 128), F32),
            pltpu.VMEM((ROWS, FPAD), F32),
            pltpu.VMEM((SLOTS, SLOTS), BF),
            pltpu.VMEM((SLOTS, FPAD), F32),
            pltpu.VMEM((3, SLOTS, FPAD), F32),
            pltpu.VMEM((2, SLOTS, FPAD), BF),
            *([slab] * 8),
            *([pltpu.VMEM((GUESTS, OBS_ROWS, FPAD), BF)] * 4),
            pltpu.VMEM((N_OBS, 8, 128), F32),
            pltpu.VMEM((N_COL, 8, 128), F32),
            dma((2, NCHUNK)),
            dma((6,)),
            dma((N_COL,)),
            dma((N_COL,)),
            dma((1, N_OBS)),
            dma((1, N_OBS)),
            dma((3, len(K_PARTS))),
            dma((3, len(K_PARTS))),
            dma((4, GUESTS)),
            dma((4, GUESTS)),
            dma((24,)),
            dma((24,)),
        ],
        compiler_params=pltpu.CompilerParams(collective_id=0, has_side_effects=True, vmem_limit_bytes=62 << 20),
        name="inner_loop",
    )(
        obs_count, channel_count, obs_owner.reshape(1, ROWS), obs_column.reshape(1, ROWS), error_inv,
        vertical.transpose(1, 0, 2), departures, jacobian,
    )
    out = jax.ShapeDtypeStruct((LEV, NVAR, COLS_DEV), F32)
    inc, res = pl.pallas_call(
        expand,
        out_shape=(out, out),
        in_specs=[hbm],
        out_specs=(hbm, hbm),
        scratch_shapes=[
            pltpu.VMEM((FPAD // 128, 2, SLOTS, 128), BF),
            pltpu.VMEM((LEV, NVAR, COLS_DEV), F32),
            pltpu.VMEM((LEV, NVAR, COLS_DEV), F32),
            dma((FPAD // 128,)),
            dma((FPAD // 128, 2)),
        ],
        compiler_params=pltpu.CompilerParams(vmem_limit_bytes=62 << 20),
        name="expand",
    )(packed)
    return inc.transpose(1, 0, 2), res.transpose(1, 0, 2)


def solution(mesh):
    in_specs = (
        P(("col", "obs"), None),
        P(("col", "obs"), None),
        P(("col", "obs")),
        P(("col", "obs")),
        P("obs"),
        P("obs", None),
        P("obs", None, None),
        P(),
    )
    out_specs = (P(None, None, ("col", "obs")), P(None, None, ("col", "obs")))
    return jax.shard_map(per_device, mesh=mesh, in_specs=in_specs, out_specs=out_specs, check_vma=False)
```

```python
import jax
import jax.numpy as jnp
from jax import lax
from jax.experimental import pallas as pl
from jax.experimental.pallas import tpu as pltpu
from jax.sharding import PartitionSpec as P

MESH = pl.DeviceIdType.MESH
BF = jnp.bfloat16
F32 = jnp.float32
COLS_DEV = 1024
NVAR, LEV = 4, 137
FEAT = NVAR * LEV
FPAD = 640
ROWS = 128
SLOTS = 256
CH = 4096
CHUNK = 1024
NCHUNK = CH // CHUNK
K_PARTS = ((0, 560, 0), (128, 432, 128), (640, 304, 0), (768, 176, 128), (1024, 48, 0))
K_FREE = ((560, 80), (944, 80), (1072, 80))
K_ROWS = 1152
GUESTS = 5
N_COL, N_OBS = 16, 8
COL_ROWS = SLOTS // N_COL
OBS_ROWS = SLOTS // N_OBS
NT = (((1,), (1,)), ((), ()))
N_CHIP = 4
CHIP_ROWS = 2 * OBS_ROWS
CHIP_ORDER = (2, 1, 3)
PLANE_ORDER = sorted(
    ((dx, dy) for dx in range(4) for dy in range(4) if dx or dy), key=lambda d: -(min(d[0], 4 - d[0]) + min(d[1], 4 - d[1]))
)


def iota(shape, axis):
    return lax.broadcasted_iota(jnp.int32, shape, axis)


def total(value):
    return jnp.sum(jnp.sum(value, axis=0, keepdims=True), axis=1, keepdims=True)


def inner_loop(
    count_hbm, channels_hbm, owner_hbm, column_hbm, error_hbm, vertical_hbm, dep_hbm, jac_hbm,
    out,
    obs_count, channel_count, owner, column, error_inv, vertical, dep, jac, lift, lift_low, gram, gram_low, kern, kacc,
    same, full1, wide, split, sent, held, queued, rows0, prof0, rows1, prof1, rows2, guest0, reply0, guest1, reply1, tile_a, tile_b,
    in_sem, small_sem, col_send, col_recv, obs_send, obs_recv, kern_send, kern_recv, leg_send, leg_recv, sum_send, sum_recv,
):
    col, obs = lax.axis_index("col"), lax.axis_index("obs")
    chip, core = obs // 2, lax.rem(obs, 2)
    sibling = chip * 2 + 1 - core
    col_x, col_y = col // 4, lax.rem(col, 4)
    plane = [lax.rem(col_x + dx, 4) * 4 + lax.rem(col_y + dy, 4) for dx, dy in PLANE_ORDER]
    small = [
        pltpu.make_async_copy(source, target, small_sem.at[index])
        for index, (source, target) in enumerate((
            (vertical_hbm, vertical), (error_hbm, error_inv), (owner_hbm, owner), (column_hbm, column),
            (count_hbm, obs_count), (channels_hbm, channel_count),
        ))
    ]
    for copy in small:
        copy.start()

    def load(chunk):
        lanes = pl.ds(pl.multiple_of(chunk * CHUNK, CHUNK), CHUNK)
        return (
            pltpu.make_async_copy(jac_hbm.at[0, :, lanes], jac.at[chunk], in_sem.at[0, chunk]),
            pltpu.make_async_copy(dep_hbm.at[:, lanes], dep.at[chunk], in_sem.at[1, chunk]),
        )

    for chunk in range(NCHUNK):
        for copy in load(chunk):
            copy.start()

    barrier = pltpu.get_barrier_semaphore()
    for step in range(1, N_OBS):
        pl.semaphore_signal(barrier, inc=1, device_id={"obs": lax.rem(obs + step, N_OBS)}, device_id_type=MESH)
    for step in range(1, N_COL):
        pl.semaphore_signal(barrier, inc=1, device_id={"col": lax.rem(col + step, N_COL)}, device_id_type=MESH)

    for copy in small[1:]:
        copy.wait()

    owner_lanes = jnp.broadcast_to(owner[...].astype(F32), (ROWS, ROWS))
    owner_rows = owner_lanes.T
    earlier = jnp.where((owner_lanes == owner_rows) & (iota((ROWS, ROWS), 0) < iota((ROWS, ROWS), 1)), 1.0, 0.0)
    slot = owner[...] * 2 + jnp.sum(earlier, axis=0, keepdims=True).astype(jnp.int32)
    live_lanes = iota((1, ROWS), 1) < obs_count[0]
    place = jnp.where((iota((SLOTS, ROWS), 0) == slot) & live_lanes, 1.0, 0.0).astype(BF)
    column_rows = jnp.broadcast_to(column[...].astype(F32), (ROWS, ROWS)).T[:, 0:1]
    column_high = jnp.floor(column_rows * (1.0 / 32.0))
    column_low = column_rows - 32.0 * column_high

    def weights(chunk):
        lanes = pl.ds(pl.multiple_of(chunk * CHUNK, CHUNK), CHUNK)
        channel = chunk * CHUNK + iota((1, CHUNK), 1)
        return jnp.where(channel < channel_count[0], error_inv[:, lanes], 0.0)

    kacc[...] = jnp.zeros_like(kacc)

    def kern_chunk(chunk, top, acc):
        count = min(256, FEAT - top)
        scaled = (jac[chunk, top : top + count, :].astype(F32) * weights(chunk)).astype(BF)
        acc[0 : FEAT - top, 0:count] += lax.dot_general(jac[chunk, top:FEAT, :], scaled, NT, preferred_element_type=F32)

    def first_chunk(chunk, carry):
        for copy in load(chunk):
            copy.wait()
        weight = weights(chunk)
        beside = jnp.concatenate(
            [(jac[chunk, 0:256, :].astype(F32) * weight).astype(BF), (weight * dep[chunk]).astype(BF)], axis=0
        )
        kacc[0:FEAT, :] += lax.dot_general(jac[chunk], beside, NT, preferred_element_type=F32)
        return carry

    lax.fori_loop(0, NCHUNK, first_chunk, 0)
    lane = iota((ROWS, 128), 1)
    extras = jnp.where(lane == FEAT - 512, column_high, 0.0)
    extras = jnp.where(lane == FEAT + 1 - 512, column_low, extras)
    extras = jnp.where(lane == FEAT + 2 - 512, 1.0, extras).astype(BF)
    placed = lax.dot_general(place, kacc[:, 256:384].astype(BF), NT, preferred_element_type=F32)
    tail = placed[:, 512:640] + jnp.dot(place, extras, preferred_element_type=F32)
    sent[...] = jnp.concatenate([placed[:, 0:512], tail], axis=1).astype(BF)

    pl.semaphore_wait(barrier, N_OBS - 1 + N_COL - 1)

    def block(index, size):
        return pl.ds(pl.multiple_of(index * size, size), size)

    col_copies = []
    for step, other in enumerate(plane):
        copy = pltpu.make_async_remote_copy(
            src_ref=sent.at[block(other, COL_ROWS)], dst_ref=held.at[block(col, COL_ROWS)],
            send_sem=col_send.at[step], recv_sem=col_recv.at[step],
            device_id={"col": other}, device_id_type=MESH,
        )
        copy.start()
        col_copies.append(copy)
    held[block(col, COL_ROWS), :] = sent[block(col, COL_ROWS), :]

    for first, count in K_FREE:
        kern[:, first : first + count, :] = jnp.zeros((3, count, 256), BF)
    kern_copies = []
    diagonal = iota((256, 256), 0) == iota((256, 256), 1)

    def kern_part(which, index):
        first, count, lane_at = K_PARTS[index]
        return kern.at[which, pl.ds(first, count), pl.ds(lane_at, 128)]

    def send_kern(parts):
        for index in parts:
            for target, away in ((0, 1), (2, 3)):
                copy = pltpu.make_async_remote_copy(
                    src_ref=kern_part(1, index), dst_ref=kern_part(target, index),
                    send_sem=kern_send.at[target, index], recv_sem=kern_recv.at[target, index],
                    device_id={"obs": lax.rem(chip + away, N_CHIP) * 2 + core}, device_id_type=MESH,
                )
                copy.start()
                kern_copies.append(copy)

    def fill_kern(which):
        for first in (0, 640):
            kern[which, first : first + 128, 128:256] = kern[which, first + 128 : first + 256, 0:128].astype(F32).T.astype(BF)

    corner = kacc[0:256, 0:256]
    shift = (total(jnp.where(diagonal, corner, 0.0)) * (1.0 / 256)).astype(BF).astype(F32)
    kern[1, 0:256, :] = jnp.where(diagonal, corner - shift, corner).astype(BF)
    kern[1, 256:560, :] = kacc[256:560, 0:256].astype(BF)
    send_kern((0, 1))
    for first, top in ((640, 256), (1024, 512)):
        kacc[0:304, 0:256] = jnp.zeros((304, 256), F32)

        def more_chunk(chunk, carry):
            kern_chunk(chunk, top, kacc)
            return carry

        lax.fori_loop(0, NCHUNK, more_chunk, 0)
        corner = kacc[0:256, 0:256]
        corner = jnp.where(diagonal, corner - shift, corner)
        if top == 256:
            kern[1, first : first + 256, :] = corner.astype(BF)
            kern[1, first + 256 : first + 304, :] = kacc[256:304, 0:256].astype(BF)
        else:
            kern[1, first : first + 48, 0:128] = jnp.where(iota((48, 128), 0) < FEAT - top, corner[0:48, 0:128], shift).astype(BF)

    for copy in col_copies:
        copy.wait_recv()

    target, source = iota((SLOTS, SLOTS), 0), iota((SLOTS, SLOTS), 1)
    wanted = lax.rem(target // 2, N_COL) * COL_ROWS + (target // OBS_ROWS) * 2 + lax.rem(target, 2)
    turn = jnp.where(source == wanted, 1.0, 0.0).astype(BF)
    queued[...] = jnp.dot(turn, held[...], preferred_element_type=F32).astype(BF)

    sends = []

    def rows_to(number, away, source_ref, target_ref):
        there = lax.rem(chip + away, N_CHIP)
        if away == 0:
            target_ref[block(obs, OBS_ROWS), :] = source_ref[block(obs, OBS_ROWS), :]
            others = ((1, sibling),)
        else:
            others = ((0, there * 2 + core), (1, there * 2 + 1 - core))
        for which, other in others:
            copy = pltpu.make_async_remote_copy(
                src_ref=source_ref.at[block(other, OBS_ROWS)], dst_ref=target_ref.at[block(obs, OBS_ROWS)],
                send_sem=obs_send.at[number, 2 * away + which], recv_sem=obs_recv.at[number, 2 * away + which],
                device_id={"obs": other}, device_id_type=MESH,
            )
            copy.start()
            sends.append(copy)

    def rows_from(number, away, target_ref):
        there = lax.rem(chip + N_CHIP - away, N_CHIP)
        others = ((1, sibling),) if away == 0 else ((0, there * 2 + core), (1, there * 2 + 1 - core))
        for which, other in others:
            pltpu.make_async_remote_copy(
                src_ref=target_ref.at[block(other, OBS_ROWS)], dst_ref=target_ref.at[block(other, OBS_ROWS)],
                send_sem=obs_send.at[number, 2 * away + which], recv_sem=obs_recv.at[number, 2 * away + which],
                device_id={"obs": other}, device_id_type=MESH,
            ).wait_recv()
        return block(there, CHIP_ROWS)

    for away in (*CHIP_ORDER, 0):
        rows_to(0, away, queued, rows0)
    send_kern((2, 3, 4))
    lift[...] = jnp.zeros_like(lift)
    small[0].wait()
    for var in range(NVAR):
        lift[var * LEV : (var + 1) * LEV, var * 256 : var * 256 + LEV] = vertical[:, var, :]
    gram[...] = jnp.zeros_like(gram)
    for var in range(NVAR):
        part = lift[var * 128 : var * 128 + 256, var * 256 : var * 256 + 256]
        square = lax.dot_general(part, part, NT, precision=lax.Precision.HIGHEST, preferred_element_type=F32)
        where = slice(var * 128, var * 128 + 256)
        gram[where, where] = gram[where, where] + square

    gram_low[...] = gram[...].astype(BF)
    lane_of = iota((256, FPAD), 1)
    for var in range(NVAR):
        turned = jnp.where(lane_of == iota((256, FPAD), 0) * NVAR + var, 1.0, 0.0).astype(BF)
        part = lift[var * 128 : var * 128 + 256, var * 256 : var * 256 + 256].astype(BF)
        placed = jnp.dot(part, turned, preferred_element_type=F32).astype(BF)
        if var == 0:
            lift_low[0:256] = placed
        else:
            lift_low[var * 128 : var * 128 + 128] += placed[0:128]
            lift_low[var * 128 + 128 : var * 128 + 256] = placed[128:256]

    for away in (0, *CHIP_ORDER):
        rows_from(0, away, rows0)

    extra = rows0[:, 512:640].astype(F32)
    extra_lanes = extra.T
    at = FEAT - 512
    live = extra[:, at + 2 : at + 3]
    column_of = jnp.where(live > 0.5, extra[:, at : at + 1] * 32.0 + extra[:, at + 1 : at + 2], -1.0)
    column_across = jnp.where(
        extra_lanes[at + 2 : at + 3, :] > 0.5,
        extra_lanes[at : at + 1, :] * 32.0 + extra_lanes[at + 1 : at + 2, :],
        -2.0,
    )
    same[...] = jnp.where(column_of == column_across, 1.0, 0.0).astype(BF)

    def halves(value):
        high = value.astype(BF)
        return high, (value - high.astype(F32)).astype(BF)

    def send_profiles(number, gathered, prof_ref, target_ref, own):
        high, low = halves(gathered)
        split[0] = high
        split[1] = low
        moment = jnp.zeros((1, 1), F32)
        products = []
        for away in (*CHIP_ORDER, 0):
            here = block(lax.rem(chip + away, N_CHIP), CHIP_ROWS)
            pair = jnp.concatenate([split[0, here, :], split[1, here, :]], axis=0)
            both = jnp.dot(pair, gram_low[...], preferred_element_type=F32)
            lifted = both[0:CHIP_ROWS] + both[CHIP_ROWS:]
            prof_ref[here, :] = lifted.astype(BF)
            profiles_to(number, away, prof_ref, target_ref)
            products.append((lifted, here))
        for lifted, here in products:
            moment += total(lifted * own[here, :].astype(F32))
        return moment

    def slab(chip_index, core_index):
        return block(lax.rem(chip_index, N_CHIP) * 2 + core_index, OBS_ROWS)

    def copy_of(number, source, target, send, recv, device):
        return pltpu.make_async_remote_copy(
            src_ref=source, dst_ref=target, send_sem=leg_send.at[number, send], recv_sem=leg_recv.at[number, recv],
            device_id={"obs": device}, device_id_type=MESH,
        )

    helper = lax.rem(chip + 1 + 2 * core, N_CHIP)

    def go(copy):
        copy.start()
        sends.append(copy)

    def profiles_to(number, away, prof_ref, guest_ref):
        if away == 2:
            for other in range(2):
                go(copy_of(number, prof_ref.at[slab(chip + 2, other)], guest_ref.at[4 - core], 3 + other, 4 - core, helper * 2 + other))
        else:
            slot = (away + 1) % N_CHIP
            go(copy_of(number, prof_ref.at[slab(chip + away, 1 - core)], guest_ref.at[slot], slot, slot, sibling))

    def apply_kern(number, prof_ref, guest_ref, reply_ref, target_ref, after):
        moment = jnp.zeros((1, 1), F32)
        for which, guests in ((1, (1,)), (0, (3, 0)), (2, (4, 2))):
            own = slab(chip + which + 3, core)
            for guest in guests:
                copy_of(number, guest_ref.at[guest], guest_ref.at[guest], guest, guest, sibling).wait_recv()
            if number == 0 and which != 1:
                for index in range(len(K_PARTS)):
                    part = kern_part(which, index)
                    pltpu.make_async_remote_copy(
                        src_ref=part, dst_ref=part, send_sem=kern_send.at[which, index], recv_sem=kern_recv.at[which, index],
                        device_id={"obs": sibling}, device_id_type=MESH,
                    ).wait_recv()
                fill_kern(which)
            profiles = jnp.concatenate([prof_ref[own, :]] + [guest_ref[guest] for guest in guests], axis=0)
            left, middle, right = profiles[:, 0:256], profiles[:, 256:512], profiles[:, 512:640]
            dot = lambda one, two: jnp.dot(one, two, preferred_element_type=F32)
            dot_turned = lambda one, two: lax.dot_general(one, two, NT, preferred_element_type=F32)
            adjoint = jnp.concatenate(
                [
                    dot(profiles, kern[which, 0:640, :]),
                    dot_turned(left, kern[which, 256:512, :]) + dot(profiles[:, 256:640], kern[which, 640:1024, :]),
                    dot_turned(left, kern[which, 512:640, :]) + dot_turned(middle, kern[which, 896:1024, :])
                    + dot(right, kern[which, 1024:1152, 0:128]),
                ],
                axis=1,
            )
            away_shift = kern[which, 1056:1072, 0:128].astype(F32)[8:9, 0:1]
            rows_out = jnp.where(iota(adjoint.shape, 1) == FEAT, away_shift, adjoint).astype(BF)
            target_ref[own, :] = rows_out[0:OBS_ROWS]
            for index, guest in enumerate(guests):
                reply_ref[guest] = rows_out[(index + 1) * OBS_ROWS : (index + 2) * OBS_ROWS]

            def answer():
                for guest in guests:
                    if guest < 3:
                        go(copy_of(number + 1, reply_ref.at[guest], target_ref.at[own], guest, guest, sibling))
                    else:
                        back = lax.rem(chip + (1 if guest == 3 else 3), N_CHIP) * 2 + (1 if guest == 3 else 0)
                        go(copy_of(number + 1, reply_ref.at[guest], target_ref.at[own], guest, 3 + core, back))

            last = after is not None and which == 2
            if not last:
                answer()
            profiles = profiles.astype(F32)
            moment += total(profiles * (adjoint + away_shift * profiles))
            if last:
                after(moment)
                answer()
        return moment

    def replies(number, target_ref):
        for slot in range(3):
            here = target_ref.at[slab(chip + slot + 3, 1 - core)]
            copy_of(number, here, here, slot, slot, sibling).wait_recv()
        for other in range(2):
            here = target_ref.at[slab(chip + 2, other)]
            copy_of(number, here, here, 3 + other, 3 + other, sibling).wait_recv()

    def whole(adj_ref, prof_ref):
        adjoint = adj_ref[...].astype(F32)
        shifts = adjoint[:, FEAT : FEAT + 1]
        return jnp.where(iota((SLOTS, FPAD), 1) < FEAT, adjoint + shifts * prof_ref[...].astype(F32), 0.0)

    gathered = jnp.dot(same[...], rows0[...], preferred_element_type=F32)
    moment0 = send_profiles(0, gathered, prof0, guest0, rows0)
    moment1 = apply_kern(0, prof0, guest0, reply0, rows1, None)
    replies(1, rows1)
    full1[...] = whole(rows1, prof0)
    high, low = halves(full1[...])
    gathered = jnp.dot(same[...], high, preferred_element_type=F32) + jnp.dot(same[...], low, preferred_element_type=F32)
    moment2 = send_profiles(2, gathered, prof1, guest1, full1)

    row = iota((8, 128), 0)
    sums = []

    def send_moments(moment3):
        tile_a[obs] = jnp.where(
            row == 0, moment0, jnp.where(row == 1, moment1, jnp.where(row == 2, moment2, jnp.where(row == 3, moment3, 0.0)))
        )
        for step in (4, 5, 3, 2, 6, 7, 1):
            copy = pltpu.make_async_remote_copy(
                src_ref=tile_a.at[obs], dst_ref=tile_a.at[obs], send_sem=sum_send.at[step], recv_sem=sum_recv.at[step],
                device_id={"obs": lax.rem(obs + step, N_OBS)}, device_id_type=MESH,
            )
            copy.start()
            sums.append(copy)

    apply_kern(2, prof1, guest1, reply1, rows2, send_moments)
    for copy in sums:
        copy.wait_recv()
    tile_b[col] = jnp.sum(tile_a[...], axis=0)
    sums_col = []
    for step, other in enumerate(plane):
        copy = pltpu.make_async_remote_copy(
            src_ref=tile_b.at[col], dst_ref=tile_b.at[col], send_sem=sum_send.at[8 + step], recv_sem=sum_recv.at[8 + step],
            device_id={"col": other}, device_id_type=MESH,
        )
        copy.start()
        sums_col.append(copy)
    replies(3, rows2)
    wide[0] = jnp.dot(rows0[...], lift_low[...], preferred_element_type=F32)
    high, low = halves(full1[...])
    wide[1] = jnp.dot(high, lift_low[...], preferred_element_type=F32) + jnp.dot(low, lift_low[...], preferred_element_type=F32)
    high, low = halves(whole(rows2, prof1))
    wide[2] = jnp.dot(high, lift_low[...], preferred_element_type=F32) + jnp.dot(low, lift_low[...], preferred_element_type=F32)
    for copy in sums_col:
        copy.wait_recv()
    moments = jnp.sum(tile_b[...], axis=0)
    m0, m1, m2, m3 = (moments[index : index + 1, 0:1] for index in range(4))

    step0 = m0 / (m0 + m1)
    rest = 1.0 - step0
    norm1 = rest * rest * m0 - 2.0 * step0 * rest * m1 + step0 * step0 * m2
    dir0, dir1 = rest + norm1 / m0, -step0
    curve = dir0 * dir0 * m0 + (dir0 * (dir0 + dir1) + dir0 * dir1) * m1 + (dir0 * dir1 + dir1 * (dir0 + dir1)) * m2 + dir1 * dir1 * m3
    step1 = norm1 / curve
    tail = iota((SLOTS, FPAD), 1) >= FEAT
    inc = (step0 + step1 * dir0) * wide[0] + (step1 * dir1) * wide[1]
    res = (rest - step1 * dir0) * wide[0] - (step0 + step1 * (dir0 + dir1)) * wide[1] - (step1 * dir1) * wide[2]
    out[0] = jnp.where(tail, rows0[...].astype(F32), inc).astype(BF)
    out[1] = jnp.where(tail, 0.0, res).astype(BF)

    for copy in (*col_copies, *kern_copies, *sends, *sums, *sums_col):
        copy.wait_send()


def expand(packed, out_inc, out_res, taken, full_inc, full_res, in_sem, out_sem):
    parts = FPAD // 128
    levels = 128 // NVAR
    order = (parts - 1, *range(parts - 1))
    loads = [
        pltpu.make_async_copy(packed.at[:, :, pl.ds(128 * part, 128)], taken.at[part], in_sem.at[part]) for part in range(parts)
    ]
    for part in order:
        loads[part].start()
    loads[parts - 1].wait()
    extra = taken[parts - 1, 0].astype(F32)
    at = FEAT - 512
    column_of = jnp.where(extra[:, at + 2 : at + 3] > 0.5, extra[:, at : at + 1] * 32.0 + extra[:, at + 1 : at + 2], -1.0)
    hit = jnp.where(column_of.astype(jnp.int32) == iota((SLOTS, COLS_DEV), 1), 1.0, 0.0).astype(BF)
    contract = (((0,), (0,)), ((), ()))
    stores = []
    for part in order:
        if part < parts - 1:
            loads[part].wait()
        count = min(levels, LEV - levels * part)
        for index, (full, out) in enumerate(((full_inc, out_inc), (full_res, out_res))):
            values = lax.dot_general(taken[part, index], hit, contract, preferred_element_type=F32)
            full[levels * part : levels * part + count] = values[0 : NVAR * count].reshape(count, NVAR, COLS_DEV)
            here = pl.ds(levels * part, count)
            store = pltpu.make_async_copy(full.at[here], out.at[here], out_sem.at[part, index])
            store.start()
            stores.append(store)
    for store in stores:
        store.wait()


def per_device(departures, obs_owner, obs_column, obs_count, channel_count, error_inv, jacobian, vertical):
    vmem, hbm = pl.BlockSpec(memory_space=pltpu.VMEM), pl.BlockSpec(memory_space=pltpu.HBM)
    dma = pltpu.SemaphoreType.DMA
    slab = pltpu.VMEM((SLOTS, FPAD), BF)
    packed = pl.pallas_call(
        inner_loop,
        out_shape=jax.ShapeDtypeStruct((2, SLOTS, FPAD), BF),
        in_specs=[hbm] * 8,
        out_specs=vmem,
        scratch_shapes=[
            pltpu.SMEM((1,), jnp.int32),
            pltpu.SMEM((1,), jnp.int32),
            pltpu.VMEM((1, ROWS), jnp.int32),
            pltpu.VMEM((1, ROWS), jnp.int32),
            pltpu.VMEM((1, CH), F32),
            pltpu.VMEM((LEV, NVAR, LEV), F32),
            pltpu.VMEM((NCHUNK, ROWS, CHUNK), F32),
            pltpu.VMEM((NCHUNK, FEAT, CHUNK), BF),
            pltpu.VMEM((FPAD, NVAR * 256), F32),
            pltpu.VMEM((FPAD, FPAD), BF),
            pltpu.VMEM((FPAD, FPAD), F32),
            pltpu.VMEM((FPAD, FPAD), BF),
            pltpu.VMEM((3, K_ROWS, 256), BF),
            pltpu.VMEM((FPAD, 384), F32),
            pltpu.VMEM((SLOTS, SLOTS), BF),
            pltpu.VMEM((SLOTS, FPAD), F32),
            pltpu.VMEM((3, SLOTS, FPAD), F32),
            pltpu.VMEM((2, SLOTS, FPAD), BF),
            *([slab] * 8),
            *([pltpu.VMEM((GUESTS, OBS_ROWS, FPAD), BF)] * 4),
            pltpu.VMEM((N_OBS, 8, 128), F32),
            pltpu.VMEM((N_COL, 8, 128), F32),
            dma((2, NCHUNK)),
            dma((6,)),
            dma((N_COL,)),
            dma((N_COL,)),
            dma((1, N_OBS)),
            dma((1, N_OBS)),
            dma((3, len(K_PARTS))),
            dma((3, len(K_PARTS))),
            dma((4, GUESTS)),
            dma((4, GUESTS)),
            dma((24,)),
            dma((24,)),
        ],
        compiler_params=pltpu.CompilerParams(collective_id=0, has_side_effects=True, vmem_limit_bytes=62 << 20),
        name="inner_loop",
    )(
        obs_count, channel_count, obs_owner.reshape(1, ROWS), obs_column.reshape(1, ROWS), error_inv,
        vertical.transpose(1, 0, 2), departures, jacobian,
    )
    out = jax.ShapeDtypeStruct((LEV, NVAR, COLS_DEV), F32)
    inc, res = pl.pallas_call(
        expand,
        out_shape=(out, out),
        in_specs=[hbm],
        out_specs=(hbm, hbm),
        scratch_shapes=[
            pltpu.VMEM((FPAD // 128, 2, SLOTS, 128), BF),
            pltpu.VMEM((LEV, NVAR, COLS_DEV), F32),
            pltpu.VMEM((LEV, NVAR, COLS_DEV), F32),
            dma((FPAD // 128,)),
            dma((FPAD // 128, 2)),
        ],
        compiler_params=pltpu.CompilerParams(vmem_limit_bytes=62 << 20),
        name="expand",
    )(packed)
    return inc.transpose(1, 0, 2), res.transpose(1, 0, 2)


def solution(mesh):
    in_specs = (
        P(("col", "obs"), None),
        P(("col", "obs"), None),
        P(("col", "obs")),
        P(("col", "obs")),
        P("obs"),
        P("obs", None),
        P("obs", None, None),
        P(),
    )
    out_specs = (P(None, None, ("col", "obs")), P(None, None, ("col", "obs")))
    return jax.shard_map(per_device, mesh=mesh, in_specs=in_specs, out_specs=out_specs, check_vma=False)
```

```python
import jax
import jax.numpy as jnp
from jax import lax
from jax.experimental import pallas as pl
from jax.experimental.pallas import tpu as pltpu
from jax.sharding import PartitionSpec as P

MESH = pl.DeviceIdType.MESH
BF = jnp.bfloat16
F32 = jnp.float32
COLS_DEV = 1024
NVAR, LEV = 4, 137
FEAT = NVAR * LEV
FPAD = 640
ROWS = 128
SLOTS = 256
CH = 4096
CHUNK = 1024
NCHUNK = CH // CHUNK
K_PARTS = ((0, 560, 0), (128, 432, 128), (640, 304, 0), (768, 176, 128), (1024, 48, 0))
K_FREE = ((560, 80), (944, 80), (1072, 80))
K_ROWS = 1152
GUESTS = 5
N_COL, N_OBS = 16, 8
COL_ROWS = SLOTS // N_COL
OBS_ROWS = SLOTS // N_OBS
NT = (((1,), (1,)), ((), ()))
N_CHIP = 4
CHIP_ROWS = 2 * OBS_ROWS
CHIP_ORDER = (2, 1, 3)
PLANE_ORDER = sorted(
    ((dx, dy) for dx in range(4) for dy in range(4) if dx or dy), key=lambda d: -(min(d[0], 4 - d[0]) + min(d[1], 4 - d[1]))
)


def iota(shape, axis):
    return lax.broadcasted_iota(jnp.int32, shape, axis)


def total(value):
    return jnp.sum(jnp.sum(value, axis=0, keepdims=True), axis=1, keepdims=True)


def inner_loop(
    count_hbm, channels_hbm, owner_hbm, column_hbm, error_hbm, vertical_hbm, dep_hbm, jac_hbm,
    out,
    obs_count, channel_count, owner, column, error_inv, vertical, dep, jac, lift, lift_low, gram, gram_low, kern, kacc,
    same, full1, wide, split, sent, held, queued, rows0, prof0, rows1, prof1, rows2, guest0, reply0, guest1, reply1, tile_a, tile_b,
    in_sem, small_sem, col_send, col_recv, obs_send, obs_recv, kern_send, kern_recv, leg_send, leg_recv, sum_send, sum_recv,
):
    col, obs = lax.axis_index("col"), lax.axis_index("obs")
    chip, core = obs // 2, lax.rem(obs, 2)
    sibling = chip * 2 + 1 - core
    col_x, col_y = col // 4, lax.rem(col, 4)
    plane = [lax.rem(col_x + dx, 4) * 4 + lax.rem(col_y + dy, 4) for dx, dy in PLANE_ORDER]
    small = [
        pltpu.make_async_copy(source, target, small_sem.at[index])
        for index, (source, target) in enumerate((
            (vertical_hbm, vertical), (error_hbm, error_inv), (owner_hbm, owner), (column_hbm, column),
            (count_hbm, obs_count), (channels_hbm, channel_count),
        ))
    ]
    for copy in small:
        copy.start()

    def load(chunk):
        lanes = pl.ds(pl.multiple_of(chunk * CHUNK, CHUNK), CHUNK)
        return (
            pltpu.make_async_copy(jac_hbm.at[0, :, lanes], jac.at[chunk], in_sem.at[0, chunk]),
            pltpu.make_async_copy(dep_hbm.at[:, lanes], dep.at[chunk], in_sem.at[1, chunk]),
        )

    for chunk in range(NCHUNK):
        for copy in load(chunk):
            copy.start()

    barrier = pltpu.get_barrier_semaphore()
    for step in range(1, N_OBS):
        pl.semaphore_signal(barrier, inc=1, device_id={"obs": lax.rem(obs + step, N_OBS)}, device_id_type=MESH)
    for step in range(1, N_COL):
        pl.semaphore_signal(barrier, inc=1, device_id={"col": lax.rem(col + step, N_COL)}, device_id_type=MESH)

    for copy in small[1:]:
        copy.wait()

    owner_lanes = jnp.broadcast_to(owner[...].astype(F32), (ROWS, ROWS))
    owner_rows = owner_lanes.T
    earlier = jnp.where((owner_lanes == owner_rows) & (iota((ROWS, ROWS), 0) < iota((ROWS, ROWS), 1)), 1.0, 0.0)
    slot = owner[...] * 2 + jnp.sum(earlier, axis=0, keepdims=True).astype(jnp.int32)
    live_lanes = iota((1, ROWS), 1) < obs_count[0]
    place = jnp.where((iota((SLOTS, ROWS), 0) == slot) & live_lanes, 1.0, 0.0).astype(BF)
    column_rows = jnp.broadcast_to(column[...].astype(F32), (ROWS, ROWS)).T[:, 0:1]
    column_high = jnp.floor(column_rows * (1.0 / 32.0))
    column_low = column_rows - 32.0 * column_high

    def weights(chunk):
        lanes = pl.ds(pl.multiple_of(chunk * CHUNK, CHUNK), CHUNK)
        channel = chunk * CHUNK + iota((1, CHUNK), 1)
        return jnp.where(channel < channel_count[0], error_inv[:, lanes], 0.0)

    kacc[...] = jnp.zeros_like(kacc)

    def kern_chunk(chunk, top, acc):
        count = min(256, FEAT - top)
        scaled = (jac[chunk, top : top + count, :].astype(F32) * weights(chunk)).astype(BF)
        acc[0 : FEAT - top, 0:count] += lax.dot_general(jac[chunk, top:FEAT, :], scaled, NT, preferred_element_type=F32)

    def first_chunk(chunk, carry):
        for copy in load(chunk):
            copy.wait()
        weight = weights(chunk)
        beside = jnp.concatenate(
            [(jac[chunk, 0:128, :].astype(F32) * weight).astype(BF), (weight * dep[chunk]).astype(BF)], axis=0
        )
        kacc[0:FEAT, :] += lax.dot_general(jac[chunk], beside, NT, preferred_element_type=F32)
        return carry

    lax.fori_loop(0, NCHUNK, first_chunk, 0)
    lane = iota((ROWS, 128), 1)
    extras = jnp.where(lane == FEAT - 512, column_high, 0.0)
    extras = jnp.where(lane == FEAT + 1 - 512, column_low, extras)
    extras = jnp.where(lane == FEAT + 2 - 512, 1.0, extras).astype(BF)
    placed = lax.dot_general(place, kacc[:, 128:256].astype(BF), NT, preferred_element_type=F32)
    tail = placed[:, 512:640] + jnp.dot(place, extras, preferred_element_type=F32)
    sent[...] = jnp.concatenate([placed[:, 0:512], tail], axis=1).astype(BF)

    pl.semaphore_wait(barrier, N_OBS - 1 + N_COL - 1)

    def block(index, size):
        return pl.ds(pl.multiple_of(index * size, size), size)

    col_copies = []
    for step, other in enumerate(plane):
        copy = pltpu.make_async_remote_copy(
            src_ref=sent.at[block(other, COL_ROWS)], dst_ref=held.at[block(col, COL_ROWS)],
            send_sem=col_send.at[step], recv_sem=col_recv.at[step],
            device_id={"col": other}, device_id_type=MESH,
        )
        copy.start()
        col_copies.append(copy)
    held[block(col, COL_ROWS), :] = sent[block(col, COL_ROWS), :]

    for first, count in K_FREE:
        kern[:, first : first + count, :] = jnp.zeros((3, count, 256), BF)
    kern_copies = []
    diagonal = iota((256, 256), 0) == iota((256, 256), 1)

    def kern_part(which, index):
        first, count, lane_at = K_PARTS[index]
        return kern.at[which, pl.ds(first, count), pl.ds(lane_at, 128)]

    def send_kern(parts):
        for index in parts:
            for target, away in ((0, 1), (2, 3)):
                copy = pltpu.make_async_remote_copy(
                    src_ref=kern_part(1, index), dst_ref=kern_part(target, index),
                    send_sem=kern_send.at[target, index], recv_sem=kern_recv.at[target, index],
                    device_id={"obs": lax.rem(chip + away, N_CHIP) * 2 + core}, device_id_type=MESH,
                )
                copy.start()
                kern_copies.append(copy)

    def fill_kern(which):
        for first in (0, 640):
            kern[which, first : first + 128, 128:256] = kern[which, first + 128 : first + 256, 0:128].astype(F32).T.astype(BF)

    corner = kacc[0:128, 0:128]
    diagonal_low = diagonal[0:128, 0:128]
    shift = (total(jnp.where(diagonal_low, corner, 0.0)) * (1.0 / 128)).astype(BF).astype(F32)
    kern[1, 0:128, 0:128] = jnp.where(diagonal_low, corner - shift, corner).astype(BF)
    kern[1, 128:560, 0:128] = kacc[128:560, 0:128].astype(BF)
    send_kern((0,))
    for top, rows_here in ((128, 432), (384, 176)):
        kacc[0:rows_here] = jnp.zeros((rows_here, 256), F32)

        def more_chunk(chunk, carry):
            kern_chunk(chunk, top, kacc)
            return carry

        lax.fori_loop(0, NCHUNK, more_chunk, 0)
        if top == 128:
            corner = kacc[0:256]
            corner = jnp.where(diagonal, corner - shift, corner).astype(BF)
            kern[1, 128:384, 128:256] = corner[:, 0:128]
            kern[1, 384:560, 128:256] = kacc[256:432, 0:128].astype(BF)
            kern[1, 640:768, 0:128] = corner[128:256, 128:256]
            kern[1, 768:944, 0:128] = kacc[256:432, 128:256].astype(BF)
            send_kern((1,))
        else:
            corner = kacc[0:176]
            corner = jnp.where(diagonal[0:176], corner - shift, corner)
            kern[1, 768:944, 128:256] = corner[:, 0:128].astype(BF)
            kern[1, 1024:1072, 0:128] = jnp.where(iota((48, 128), 0) < FEAT - 512, corner[128:176, 128:256], shift).astype(BF)
    fill_kern(1)

    for copy in col_copies:
        copy.wait_recv()

    target, source = iota((SLOTS, SLOTS), 0), iota((SLOTS, SLOTS), 1)
    wanted = lax.rem(target // 2, N_COL) * COL_ROWS + (target // OBS_ROWS) * 2 + lax.rem(target, 2)
    turn = jnp.where(source == wanted, 1.0, 0.0).astype(BF)
    queued[...] = jnp.dot(turn, held[...], preferred_element_type=F32).astype(BF)

    sends = []

    def rows_to(number, away, source_ref, target_ref):
        there = lax.rem(chip + away, N_CHIP)
        if away == 0:
            target_ref[block(obs, OBS_ROWS), :] = source_ref[block(obs, OBS_ROWS), :]
            others = ((1, sibling),)
        else:
            others = ((0, there * 2 + core), (1, there * 2 + 1 - core))
        for which, other in others:
            copy = pltpu.make_async_remote_copy(
                src_ref=source_ref.at[block(other, OBS_ROWS)], dst_ref=target_ref.at[block(obs, OBS_ROWS)],
                send_sem=obs_send.at[number, 2 * away + which], recv_sem=obs_recv.at[number, 2 * away + which],
                device_id={"obs": other}, device_id_type=MESH,
            )
            copy.start()
            sends.append(copy)

    def rows_from(number, away, target_ref):
        there = lax.rem(chip + N_CHIP - away, N_CHIP)
        others = ((1, sibling),) if away == 0 else ((0, there * 2 + core), (1, there * 2 + 1 - core))
        for which, other in others:
            pltpu.make_async_remote_copy(
                src_ref=target_ref.at[block(other, OBS_ROWS)], dst_ref=target_ref.at[block(other, OBS_ROWS)],
                send_sem=obs_send.at[number, 2 * away + which], recv_sem=obs_recv.at[number, 2 * away + which],
                device_id={"obs": other}, device_id_type=MESH,
            ).wait_recv()
        return block(there, CHIP_ROWS)

    for away in (*CHIP_ORDER, 0):
        rows_to(0, away, queued, rows0)
    send_kern((2, 3, 4))
    lift[...] = jnp.zeros_like(lift)
    small[0].wait()
    for var in range(NVAR):
        lift[var * LEV : (var + 1) * LEV, var * 256 : var * 256 + LEV] = vertical[:, var, :]
    gram[...] = jnp.zeros_like(gram)
    for var in range(NVAR):
        part = lift[var * 128 : var * 128 + 256, var * 256 : var * 256 + 256]
        square = lax.dot_general(part, part, NT, precision=lax.Precision.HIGHEST, preferred_element_type=F32)
        where = slice(var * 128, var * 128 + 256)
        gram[where, where] = gram[where, where] + square

    gram_low[...] = gram[...].astype(BF)
    lane_of = iota((256, FPAD), 1)
    for var in range(NVAR):
        turned = jnp.where(lane_of == iota((256, FPAD), 0) * NVAR + var, 1.0, 0.0).astype(BF)
        part = lift[var * 128 : var * 128 + 256, var * 256 : var * 256 + 256].astype(BF)
        placed = jnp.dot(part, turned, preferred_element_type=F32).astype(BF)
        if var == 0:
            lift_low[0:256] = placed
        else:
            lift_low[var * 128 : var * 128 + 128] += placed[0:128]
            lift_low[var * 128 + 128 : var * 128 + 256] = placed[128:256]

    for away in (0, *CHIP_ORDER):
        rows_from(0, away, rows0)

    extra = rows0[:, 512:640].astype(F32)
    extra_lanes = extra.T
    at = FEAT - 512
    live = extra[:, at + 2 : at + 3]
    column_of = jnp.where(live > 0.5, extra[:, at : at + 1] * 32.0 + extra[:, at + 1 : at + 2], -1.0)
    column_across = jnp.where(
        extra_lanes[at + 2 : at + 3, :] > 0.5,
        extra_lanes[at : at + 1, :] * 32.0 + extra_lanes[at + 1 : at + 2, :],
        -2.0,
    )
    same[...] = jnp.where(column_of == column_across, 1.0, 0.0).astype(BF)

    def halves(value):
        high = value.astype(BF)
        return high, (value - high.astype(F32)).astype(BF)

    def send_profiles(number, gathered, prof_ref, target_ref, own):
        high, low = halves(gathered)
        split[0] = high
        split[1] = low
        moment = jnp.zeros((1, 1), F32)
        products = []
        for away in (*CHIP_ORDER, 0):
            here = block(lax.rem(chip + away, N_CHIP), CHIP_ROWS)
            pair = jnp.concatenate([split[0, here, :], split[1, here, :]], axis=0)
            both = jnp.dot(pair, gram_low[...], preferred_element_type=F32)
            lifted = both[0:CHIP_ROWS] + both[CHIP_ROWS:]
            prof_ref[here, :] = lifted.astype(BF)
            profiles_to(number, away, prof_ref, target_ref)
            products.append((lifted, here))
        for lifted, here in products:
            moment += total(lifted * own[here, :].astype(F32))
        return moment

    def slab(chip_index, core_index):
        return block(lax.rem(chip_index, N_CHIP) * 2 + core_index, OBS_ROWS)

    def copy_of(number, source, target, send, recv, device):
        return pltpu.make_async_remote_copy(
            src_ref=source, dst_ref=target, send_sem=leg_send.at[number, send], recv_sem=leg_recv.at[number, recv],
            device_id={"obs": device}, device_id_type=MESH,
        )

    helper = lax.rem(chip + 1 + 2 * core, N_CHIP)

    def go(copy):
        copy.start()
        sends.append(copy)

    def profiles_to(number, away, prof_ref, guest_ref):
        if away == 2:
            for other in range(2):
                go(copy_of(number, prof_ref.at[slab(chip + 2, other)], guest_ref.at[4 - core], 3 + other, 4 - core, helper * 2 + other))
        else:
            slot = (away + 1) % N_CHIP
            go(copy_of(number, prof_ref.at[slab(chip + away, 1 - core)], guest_ref.at[slot], slot, slot, sibling))

    def apply_kern(number, prof_ref, guest_ref, reply_ref, target_ref, after):
        moment = jnp.zeros((1, 1), F32)
        for which, guests in ((1, (1,)), (0, (3, 0)), (2, (4, 2))):
            own = slab(chip + which + 3, core)
            for guest in guests:
                copy_of(number, guest_ref.at[guest], guest_ref.at[guest], guest, guest, sibling).wait_recv()
            if number == 0 and which != 1:
                for index in range(len(K_PARTS)):
                    part = kern_part(which, index)
                    pltpu.make_async_remote_copy(
                        src_ref=part, dst_ref=part, send_sem=kern_send.at[which, index], recv_sem=kern_recv.at[which, index],
                        device_id={"obs": sibling}, device_id_type=MESH,
                    ).wait_recv()
                fill_kern(which)
            profiles = jnp.concatenate([prof_ref[own, :]] + [guest_ref[guest] for guest in guests], axis=0)
            left, middle, right = profiles[:, 0:256], profiles[:, 256:512], profiles[:, 512:640]
            dot = lambda one, two: jnp.dot(one, two, preferred_element_type=F32)
            dot_turned = lambda one, two: lax.dot_general(one, two, NT, preferred_element_type=F32)
            adjoint = jnp.concatenate(
                [
                    dot(profiles, kern[which, 0:640, :]),
                    dot_turned(left, kern[which, 256:512, :]) + dot(profiles[:, 256:640], kern[which, 640:1024, :]),
                    dot_turned(left, kern[which, 512:640, :]) + dot_turned(middle, kern[which, 896:1024, :])
                    + dot(right, kern[which, 1024:1152, 0:128]),
                ],
                axis=1,
            )
            away_shift = kern[which, 1056:1072, 0:128].astype(F32)[8:9, 0:1]
            rows_out = jnp.where(iota(adjoint.shape, 1) == FEAT, away_shift, adjoint).astype(BF)
            target_ref[own, :] = rows_out[0:OBS_ROWS]
            for index, guest in enumerate(guests):
                reply_ref[guest] = rows_out[(index + 1) * OBS_ROWS : (index + 2) * OBS_ROWS]

            def answer():
                for guest in guests:
                    if guest < 3:
                        go(copy_of(number + 1, reply_ref.at[guest], target_ref.at[own], guest, guest, sibling))
                    else:
                        back = lax.rem(chip + (1 if guest == 3 else 3), N_CHIP) * 2 + (1 if guest == 3 else 0)
                        go(copy_of(number + 1, reply_ref.at[guest], target_ref.at[own], guest, 3 + core, back))

            last = after is not None and which == 2
            if not last:
                answer()
            profiles = profiles.astype(F32)
            moment += total(profiles * (adjoint + away_shift * profiles))
            if last:
                after(moment)
                answer()
        return moment

    def replies(number, target_ref):
        for slot in range(3):
            here = target_ref.at[slab(chip + slot + 3, 1 - core)]
            copy_of(number, here, here, slot, slot, sibling).wait_recv()
        for other in range(2):
            here = target_ref.at[slab(chip + 2, other)]
            copy_of(number, here, here, 3 + other, 3 + other, sibling).wait_recv()

    def whole(adj_ref, prof_ref):
        adjoint = adj_ref[...].astype(F32)
        shifts = adjoint[:, FEAT : FEAT + 1]
        return jnp.where(iota((SLOTS, FPAD), 1) < FEAT, adjoint + shifts * prof_ref[...].astype(F32), 0.0)

    gathered = jnp.dot(same[...], rows0[...], preferred_element_type=F32)
    moment0 = send_profiles(0, gathered, prof0, guest0, rows0)
    moment1 = apply_kern(0, prof0, guest0, reply0, rows1, None)
    replies(1, rows1)
    full1[...] = whole(rows1, prof0)
    high, low = halves(full1[...])
    gathered = jnp.dot(same[...], high, preferred_element_type=F32) + jnp.dot(same[...], low, preferred_element_type=F32)
    moment2 = send_profiles(2, gathered, prof1, guest1, full1)

    row = iota((8, 128), 0)
    sums = []

    def send_moments(moment3):
        tile_a[obs] = jnp.where(
            row == 0, moment0, jnp.where(row == 1, moment1, jnp.where(row == 2, moment2, jnp.where(row == 3, moment3, 0.0)))
        )
        for step in (4, 5, 3, 2, 6, 7, 1):
            copy = pltpu.make_async_remote_copy(
                src_ref=tile_a.at[obs], dst_ref=tile_a.at[obs], send_sem=sum_send.at[step], recv_sem=sum_recv.at[step],
                device_id={"obs": lax.rem(obs + step, N_OBS)}, device_id_type=MESH,
            )
            copy.start()
            sums.append(copy)

    apply_kern(2, prof1, guest1, reply1, rows2, send_moments)
    for copy in sums:
        copy.wait_recv()
    tile_b[col] = jnp.sum(tile_a[...], axis=0)
    sums_col = []
    for step, other in enumerate(plane):
        copy = pltpu.make_async_remote_copy(
            src_ref=tile_b.at[col], dst_ref=tile_b.at[col], send_sem=sum_send.at[8 + step], recv_sem=sum_recv.at[8 + step],
            device_id={"col": other}, device_id_type=MESH,
        )
        copy.start()
        sums_col.append(copy)
    replies(3, rows2)
    wide[0] = jnp.dot(rows0[...], lift_low[...], preferred_element_type=F32)
    high, low = halves(full1[...])
    wide[1] = jnp.dot(high, lift_low[...], preferred_element_type=F32) + jnp.dot(low, lift_low[...], preferred_element_type=F32)
    high, low = halves(whole(rows2, prof1))
    wide[2] = jnp.dot(high, lift_low[...], preferred_element_type=F32) + jnp.dot(low, lift_low[...], preferred_element_type=F32)
    for copy in sums_col:
        copy.wait_recv()
    moments = jnp.sum(tile_b[...], axis=0)
    m0, m1, m2, m3 = (moments[index : index + 1, 0:1] for index in range(4))

    step0 = m0 / (m0 + m1)
    rest = 1.0 - step0
    norm1 = rest * rest * m0 - 2.0 * step0 * rest * m1 + step0 * step0 * m2
    dir0, dir1 = rest + norm1 / m0, -step0
    curve = dir0 * dir0 * m0 + (dir0 * (dir0 + dir1) + dir0 * dir1) * m1 + (dir0 * dir1 + dir1 * (dir0 + dir1)) * m2 + dir1 * dir1 * m3
    step1 = norm1 / curve
    tail = iota((SLOTS, FPAD), 1) >= FEAT
    inc = (step0 + step1 * dir0) * wide[0] + (step1 * dir1) * wide[1]
    res = (rest - step1 * dir0) * wide[0] - (step0 + step1 * (dir0 + dir1)) * wide[1] - (step1 * dir1) * wide[2]
    out[0] = jnp.where(tail, rows0[...].astype(F32), inc).astype(BF)
    out[1] = jnp.where(tail, 0.0, res).astype(BF)

    for copy in (*col_copies, *kern_copies, *sends, *sums, *sums_col):
        copy.wait_send()


def expand(packed, out_inc, out_res, taken, full_inc, full_res, in_sem, out_sem):
    parts = FPAD // 128
    levels = 128 // NVAR
    order = (parts - 1, *range(parts - 1))
    loads = [
        pltpu.make_async_copy(packed.at[:, :, pl.ds(128 * part, 128)], taken.at[part], in_sem.at[part]) for part in range(parts)
    ]
    for part in order:
        loads[part].start()
    loads[parts - 1].wait()
    extra = taken[parts - 1, 0].astype(F32)
    at = FEAT - 512
    column_of = jnp.where(extra[:, at + 2 : at + 3] > 0.5, extra[:, at : at + 1] * 32.0 + extra[:, at + 1 : at + 2], -1.0)
    hit = jnp.where(column_of.astype(jnp.int32) == iota((SLOTS, COLS_DEV), 1), 1.0, 0.0).astype(BF)
    contract = (((0,), (0,)), ((), ()))
    stores = []
    for part in order:
        if part < parts - 1:
            loads[part].wait()
        count = min(levels, LEV - levels * part)
        for index, (full, out) in enumerate(((full_inc, out_inc), (full_res, out_res))):
            values = lax.dot_general(taken[part, index], hit, contract, preferred_element_type=F32)
            full[levels * part : levels * part + count] = values[0 : NVAR * count].reshape(count, NVAR, COLS_DEV)
            here = pl.ds(levels * part, count)
            store = pltpu.make_async_copy(full.at[here], out.at[here], out_sem.at[part, index])
            store.start()
            stores.append(store)
    for store in stores:
        store.wait()


def per_device(departures, obs_owner, obs_column, obs_count, channel_count, error_inv, jacobian, vertical):
    vmem, hbm = pl.BlockSpec(memory_space=pltpu.VMEM), pl.BlockSpec(memory_space=pltpu.HBM)
    dma = pltpu.SemaphoreType.DMA
    slab = pltpu.VMEM((SLOTS, FPAD), BF)
    packed = pl.pallas_call(
        inner_loop,
        out_shape=jax.ShapeDtypeStruct((2, SLOTS, FPAD), BF),
        in_specs=[hbm] * 8,
        out_specs=vmem,
        scratch_shapes=[
            pltpu.SMEM((1,), jnp.int32),
            pltpu.SMEM((1,), jnp.int32),
            pltpu.VMEM((1, ROWS), jnp.int32),
            pltpu.VMEM((1, ROWS), jnp.int32),
            pltpu.VMEM((1, CH), F32),
            pltpu.VMEM((LEV, NVAR, LEV), F32),
            pltpu.VMEM((NCHUNK, ROWS, CHUNK), F32),
            pltpu.VMEM((NCHUNK, FEAT, CHUNK), BF),
            pltpu.VMEM((FPAD, NVAR * 256), F32),
            pltpu.VMEM((FPAD, FPAD), BF),
            pltpu.VMEM((FPAD, FPAD), F32),
            pltpu.VMEM((FPAD, FPAD), BF),
            pltpu.VMEM((3, K_ROWS, 256), BF),
            pltpu.VMEM((FPAD, 256), F32),
            pltpu.VMEM((SLOTS, SLOTS), BF),
            pltpu.VMEM((SLOTS, FPAD), F32),
            pltpu.VMEM((3, SLOTS, FPAD), F32),
            pltpu.VMEM((2, SLOTS, FPAD), BF),
            *([slab] * 8),
            *([pltpu.VMEM((GUESTS, OBS_ROWS, FPAD), BF)] * 4),
            pltpu.VMEM((N_OBS, 8, 128), F32),
            pltpu.VMEM((N_COL, 8, 128), F32),
            dma((2, NCHUNK)),
            dma((6,)),
            dma((N_COL,)),
            dma((N_COL,)),
            dma((1, N_OBS)),
            dma((1, N_OBS)),
            dma((3, len(K_PARTS))),
            dma((3, len(K_PARTS))),
            dma((4, GUESTS)),
            dma((4, GUESTS)),
            dma((24,)),
            dma((24,)),
        ],
        compiler_params=pltpu.CompilerParams(collective_id=0, has_side_effects=True, vmem_limit_bytes=62 << 20),
        name="inner_loop",
    )(
        obs_count, channel_count, obs_owner.reshape(1, ROWS), obs_column.reshape(1, ROWS), error_inv,
        vertical.transpose(1, 0, 2), departures, jacobian,
    )
    out = jax.ShapeDtypeStruct((LEV, NVAR, COLS_DEV), F32)
    inc, res = pl.pallas_call(
        expand,
        out_shape=(out, out),
        in_specs=[hbm],
        out_specs=(hbm, hbm),
        scratch_shapes=[
            pltpu.VMEM((FPAD // 128, 2, SLOTS, 128), BF),
            pltpu.VMEM((LEV, NVAR, COLS_DEV), F32),
            pltpu.VMEM((LEV, NVAR, COLS_DEV), F32),
            dma((FPAD // 128,)),
            dma((FPAD // 128, 2)),
        ],
        compiler_params=pltpu.CompilerParams(vmem_limit_bytes=62 << 20),
        name="expand",
    )(packed)
    return inc.transpose(1, 0, 2), res.transpose(1, 0, 2)


def solution(mesh):
    in_specs = (
        P(("col", "obs"), None),
        P(("col", "obs"), None),
        P(("col", "obs")),
        P(("col", "obs")),
        P("obs"),
        P("obs", None),
        P("obs", None, None),
        P(),
    )
    out_specs = (P(None, None, ("col", "obs")), P(None, None, ("col", "obs")))
    return jax.shard_map(per_device, mesh=mesh, in_specs=in_specs, out_specs=out_specs, check_vma=False)
```

```python
import jax
import jax.numpy as jnp
from jax import lax
from jax.experimental import pallas as pl
from jax.experimental.pallas import tpu as pltpu
from jax.sharding import PartitionSpec as P

MESH = pl.DeviceIdType.MESH
BF = jnp.bfloat16
F32 = jnp.float32
COLS_DEV = 1024
NVAR, LEV = 4, 137
FEAT = NVAR * LEV
FPAD = 640
ROWS = 128
SLOTS = 256
CH = 4096
CHUNK = 1024
NCHUNK = CH // CHUNK
K_PARTS = ((0, 560, 0), (128, 432, 128), (640, 304, 0), (768, 176, 128), (1024, 48, 0))
K_FREE = ((560, 80), (944, 80), (1072, 80))
K_ROWS = 1152
GUESTS = 5
N_COL, N_OBS = 16, 8
COL_ROWS = SLOTS // N_COL
OBS_ROWS = SLOTS // N_OBS
NT = (((1,), (1,)), ((), ()))
N_CHIP = 4
CHIP_ROWS = 2 * OBS_ROWS
CHIP_ORDER = (2, 1, 3)
PLANE_ORDER = sorted(
    ((dx, dy) for dx in range(4) for dy in range(4) if dx or dy), key=lambda d: -(min(d[0], 4 - d[0]) + min(d[1], 4 - d[1]))
)


def iota(shape, axis):
    return lax.broadcasted_iota(jnp.int32, shape, axis)


def total(value):
    return jnp.sum(jnp.sum(value, axis=0, keepdims=True), axis=1, keepdims=True)


def inner_loop(
    count_hbm, channels_hbm, owner_hbm, column_hbm, error_hbm, vertical_hbm, dep_hbm, jac_hbm,
    out,
    obs_count, channel_count, owner, column, error_inv, vertical, dep, jac, lift, lift_low, gram, gram_low, kern, kacc,
    same, full1, wide, split, sent, held, queued, rows0, prof0, rows1, prof1, rows2, guest0, reply0, guest1, reply1, tile_a, tile_b,
    in_sem, small_sem, col_send, col_recv, obs_send, obs_recv, kern_send, kern_recv, leg_send, leg_recv, sum_send, sum_recv, ready, out_sem,
):
    col, obs = lax.axis_index("col"), lax.axis_index("obs")
    chip, core = obs // 2, lax.rem(obs, 2)
    sibling = chip * 2 + 1 - core
    col_x, col_y = col // 4, lax.rem(col, 4)
    plane = [lax.rem(col_x + dx, 4) * 4 + lax.rem(col_y + dy, 4) for dx, dy in PLANE_ORDER]
    small = [
        pltpu.make_async_copy(source, target, small_sem.at[index])
        for index, (source, target) in enumerate((
            (vertical_hbm, vertical), (error_hbm, error_inv), (owner_hbm, owner), (column_hbm, column),
            (count_hbm, obs_count), (channels_hbm, channel_count),
        ))
    ]
    for copy in small:
        copy.start()

    def load(chunk):
        lanes = pl.ds(pl.multiple_of(chunk * CHUNK, CHUNK), CHUNK)
        return (
            pltpu.make_async_copy(jac_hbm.at[0, :, lanes], jac.at[chunk], in_sem.at[0, chunk]),
            pltpu.make_async_copy(dep_hbm.at[:, lanes], dep.at[chunk], in_sem.at[1, chunk]),
        )

    for chunk in range(NCHUNK):
        for copy in load(chunk):
            copy.start()

    barrier = pltpu.get_barrier_semaphore()
    for step in range(1, N_OBS):
        pl.semaphore_signal(barrier, inc=1, device_id={"obs": lax.rem(obs + step, N_OBS)}, device_id_type=MESH)
    for step in range(1, N_COL):
        pl.semaphore_signal(barrier, inc=1, device_id={"col": lax.rem(col + step, N_COL)}, device_id_type=MESH)

    for copy in small[1:]:
        copy.wait()

    owner_lanes = jnp.broadcast_to(owner[...].astype(F32), (ROWS, ROWS))
    owner_rows = owner_lanes.T
    earlier = jnp.where((owner_lanes == owner_rows) & (iota((ROWS, ROWS), 0) < iota((ROWS, ROWS), 1)), 1.0, 0.0)
    slot = owner[...] * 2 + jnp.sum(earlier, axis=0, keepdims=True).astype(jnp.int32)
    live_lanes = iota((1, ROWS), 1) < obs_count[0]
    place = jnp.where((iota((SLOTS, ROWS), 0) == slot) & live_lanes, 1.0, 0.0).astype(BF)
    column_rows = jnp.broadcast_to(column[...].astype(F32), (ROWS, ROWS)).T[:, 0:1]
    column_high = jnp.floor(column_rows * (1.0 / 32.0))
    column_low = column_rows - 32.0 * column_high

    def weights(chunk):
        lanes = pl.ds(pl.multiple_of(chunk * CHUNK, CHUNK), CHUNK)
        channel = chunk * CHUNK + iota((1, CHUNK), 1)
        return jnp.where(channel < channel_count[0], error_inv[:, lanes], 0.0)

    kacc[...] = jnp.zeros_like(kacc)

    def kern_chunk(chunk, top, acc):
        count = min(256, FEAT - top)
        scaled = (jac[chunk, top : top + count, :].astype(F32) * weights(chunk)).astype(BF)
        acc[0 : FEAT - top, 0:count] += lax.dot_general(jac[chunk, top:FEAT, :], scaled, NT, preferred_element_type=F32)

    def first_chunk(chunk, carry):
        for copy in load(chunk):
            copy.wait()
        weight = weights(chunk)
        beside = jnp.concatenate(
            [(jac[chunk, 0:128, :].astype(F32) * weight).astype(BF), (weight * dep[chunk]).astype(BF)], axis=0
        )
        kacc[0:FEAT, :] += lax.dot_general(jac[chunk], beside, NT, preferred_element_type=F32)
        return carry

    lax.fori_loop(0, NCHUNK, first_chunk, 0)
    lane = iota((ROWS, 128), 1)
    extras = jnp.where(lane == FEAT - 512, column_high, 0.0)
    extras = jnp.where(lane == FEAT + 1 - 512, column_low, extras)
    extras = jnp.where(lane == FEAT + 2 - 512, 1.0, extras).astype(BF)
    placed = lax.dot_general(place, kacc[:, 128:256].astype(BF), NT, preferred_element_type=F32)
    tail = placed[:, 512:640] + jnp.dot(place, extras, preferred_element_type=F32)
    sent[...] = jnp.concatenate([placed[:, 0:512], tail], axis=1).astype(BF)

    pl.semaphore_wait(barrier, N_OBS - 1 + N_COL - 1)

    def block(index, size):
        return pl.ds(pl.multiple_of(index * size, size), size)

    col_copies = []
    for step, other in enumerate(plane):
        copy = pltpu.make_async_remote_copy(
            src_ref=sent.at[block(other, COL_ROWS)], dst_ref=held.at[block(col, COL_ROWS)],
            send_sem=col_send.at[step], recv_sem=col_recv.at[step],
            device_id={"col": other}, device_id_type=MESH,
        )
        copy.start()
        col_copies.append(copy)
    held[block(col, COL_ROWS), :] = sent[block(col, COL_ROWS), :]

    for first, count in K_FREE:
        kern[:, first : first + count, :] = jnp.zeros((3, count, 256), BF)
    kern_copies = []
    diagonal = iota((256, 256), 0) == iota((256, 256), 1)

    def kern_part(which, index):
        first, count, lane_at = K_PARTS[index]
        return kern.at[which, pl.ds(first, count), pl.ds(lane_at, 128)]

    def send_kern(parts):
        for index in parts:
            for target, away in ((0, 1), (2, 3)):
                copy = pltpu.make_async_remote_copy(
                    src_ref=kern_part(1, index), dst_ref=kern_part(target, index),
                    send_sem=kern_send.at[target, index], recv_sem=kern_recv.at[target, index],
                    device_id={"obs": lax.rem(chip + away, N_CHIP) * 2 + core}, device_id_type=MESH,
                )
                copy.start()
                kern_copies.append(copy)

    def fill_kern(which):
        for first in (0, 640):
            kern[which, first : first + 128, 128:256] = kern[which, first + 128 : first + 256, 0:128].astype(F32).T.astype(BF)

    corner = kacc[0:128, 0:128]
    diagonal_low = diagonal[0:128, 0:128]
    shift = (total(jnp.where(diagonal_low, corner, 0.0)) * (1.0 / 128)).astype(BF).astype(F32)
    kern[1, 0:128, 0:128] = jnp.where(diagonal_low, corner - shift, corner).astype(BF)
    kern[1, 128:560, 0:128] = kacc[128:560, 0:128].astype(BF)
    send_kern((0,))
    for top, rows_here in ((128, 432), (384, 176)):
        kacc[0:rows_here] = jnp.zeros((rows_here, 256), F32)

        def more_chunk(chunk, carry):
            kern_chunk(chunk, top, kacc)
            return carry

        lax.fori_loop(0, NCHUNK, more_chunk, 0)
        if top == 128:
            corner = kacc[0:256]
            corner = jnp.where(diagonal, corner - shift, corner).astype(BF)
            kern[1, 128:384, 128:256] = corner[:, 0:128]
            kern[1, 384:560, 128:256] = kacc[256:432, 0:128].astype(BF)
            kern[1, 640:768, 0:128] = corner[128:256, 128:256]
            kern[1, 768:944, 0:128] = kacc[256:432, 128:256].astype(BF)
            send_kern((1,))
        else:
            corner = kacc[0:176]
            corner = jnp.where(diagonal[0:176], corner - shift, corner)
            kern[1, 768:944, 128:256] = corner[:, 0:128].astype(BF)
            kern[1, 1024:1072, 0:128] = jnp.where(iota((48, 128), 0) < FEAT - 512, corner[128:176, 128:256], shift).astype(BF)
    fill_kern(1)

    for copy in col_copies:
        copy.wait_recv()

    target, source = iota((SLOTS, SLOTS), 0), iota((SLOTS, SLOTS), 1)
    wanted = lax.rem(target // 2, N_COL) * COL_ROWS + (target // OBS_ROWS) * 2 + lax.rem(target, 2)
    turn = jnp.where(source == wanted, 1.0, 0.0).astype(BF)
    queued[...] = jnp.dot(turn, held[...], preferred_element_type=F32).astype(BF)

    sends = []

    def rows_to(number, away, source_ref, target_ref):
        there = lax.rem(chip + away, N_CHIP)
        if away == 0:
            target_ref[block(obs, OBS_ROWS), :] = source_ref[block(obs, OBS_ROWS), :]
            others = ((1, sibling),)
        else:
            others = ((0, there * 2 + core), (1, there * 2 + 1 - core))
        for which, other in others:
            copy = pltpu.make_async_remote_copy(
                src_ref=source_ref.at[block(other, OBS_ROWS)], dst_ref=target_ref.at[block(obs, OBS_ROWS)],
                send_sem=obs_send.at[number, 2 * away + which], recv_sem=obs_recv.at[number, 2 * away + which],
                device_id={"obs": other}, device_id_type=MESH,
            )
            copy.start()
            sends.append(copy)

    def rows_from(number, away, target_ref):
        there = lax.rem(chip + N_CHIP - away, N_CHIP)
        others = ((1, sibling),) if away == 0 else ((0, there * 2 + core), (1, there * 2 + 1 - core))
        for which, other in others:
            pltpu.make_async_remote_copy(
                src_ref=target_ref.at[block(other, OBS_ROWS)], dst_ref=target_ref.at[block(other, OBS_ROWS)],
                send_sem=obs_send.at[number, 2 * away + which], recv_sem=obs_recv.at[number, 2 * away + which],
                device_id={"obs": other}, device_id_type=MESH,
            ).wait_recv()
        return block(there, CHIP_ROWS)

    for away in (*CHIP_ORDER, 0):
        rows_to(0, away, queued, rows0)
    send_kern((2, 3, 4))
    lift[...] = jnp.zeros_like(lift)
    small[0].wait()
    for var in range(NVAR):
        lift[var * LEV : (var + 1) * LEV, var * 256 : var * 256 + LEV] = vertical[:, var, :]
    gram[...] = jnp.zeros_like(gram)
    for var in range(NVAR):
        part = lift[var * 128 : var * 128 + 256, var * 256 : var * 256 + 256]
        square = lax.dot_general(part, part, NT, precision=lax.Precision.HIGHEST, preferred_element_type=F32)
        where = slice(var * 128, var * 128 + 256)
        gram[where, where] = gram[where, where] + square

    gram_low[...] = gram[...].astype(BF)
    lane_of = iota((256, FPAD), 1)
    for var in range(NVAR):
        turned = jnp.where(lane_of == iota((256, FPAD), 0) * NVAR + var, 1.0, 0.0).astype(BF)
        part = lift[var * 128 : var * 128 + 256, var * 256 : var * 256 + 256].astype(BF)
        placed = jnp.dot(part, turned, preferred_element_type=F32).astype(BF)
        if var == 0:
            lift_low[0:256] = placed
        else:
            lift_low[var * 128 : var * 128 + 128] += placed[0:128]
            lift_low[var * 128 + 128 : var * 128 + 256] = placed[128:256]

    for away in (0, *CHIP_ORDER):
        rows_from(0, away, rows0)

    extra = rows0[:, 512:640].astype(F32)
    extra_lanes = extra.T
    at = FEAT - 512
    live = extra[:, at + 2 : at + 3]
    column_of = jnp.where(live > 0.5, extra[:, at : at + 1] * 32.0 + extra[:, at + 1 : at + 2], -1.0)
    column_across = jnp.where(
        extra_lanes[at + 2 : at + 3, :] > 0.5,
        extra_lanes[at : at + 1, :] * 32.0 + extra_lanes[at + 1 : at + 2, :],
        -2.0,
    )
    same[...] = jnp.where(column_of == column_across, 1.0, 0.0).astype(BF)

    def halves(value):
        high = value.astype(BF)
        return high, (value - high.astype(F32)).astype(BF)

    def send_profiles(number, gathered, prof_ref, target_ref, own):
        high, low = halves(gathered)
        split[0] = high
        split[1] = low
        moment = jnp.zeros((1, 1), F32)
        products = []
        for away in (*CHIP_ORDER, 0):
            here = block(lax.rem(chip + away, N_CHIP), CHIP_ROWS)
            pair = jnp.concatenate([split[0, here, :], split[1, here, :]], axis=0)
            both = jnp.dot(pair, gram_low[...], preferred_element_type=F32)
            lifted = both[0:CHIP_ROWS] + both[CHIP_ROWS:]
            prof_ref[here, :] = lifted.astype(BF)
            profiles_to(number, away, prof_ref, target_ref)
            products.append((lifted, here))
        for lifted, here in products:
            moment += total(lifted * own[here, :].astype(F32))
        return moment

    def slab(chip_index, core_index):
        return block(lax.rem(chip_index, N_CHIP) * 2 + core_index, OBS_ROWS)

    def copy_of(number, source, target, send, recv, device):
        return pltpu.make_async_remote_copy(
            src_ref=source, dst_ref=target, send_sem=leg_send.at[number, send], recv_sem=leg_recv.at[number, recv],
            device_id={"obs": device}, device_id_type=MESH,
        )

    helper = lax.rem(chip + 1 + 2 * core, N_CHIP)

    def go(copy):
        copy.start()
        sends.append(copy)

    def profiles_to(number, away, prof_ref, guest_ref):
        if away == 2:
            for other in range(2):
                go(copy_of(number, prof_ref.at[slab(chip + 2, other)], guest_ref.at[4 - core], 3 + other, 4 - core, helper * 2 + other))
        else:
            slot = (away + 1) % N_CHIP
            go(copy_of(number, prof_ref.at[slab(chip + away, 1 - core)], guest_ref.at[slot], slot, slot, sibling))

    def apply_kern(number, prof_ref, guest_ref, reply_ref, target_ref, after):
        moment = jnp.zeros((1, 1), F32)
        for which, guests in ((1, (1,)), (0, (3, 0)), (2, (4, 2))):
            own = slab(chip + which + 3, core)
            for guest in guests:
                copy_of(number, guest_ref.at[guest], guest_ref.at[guest], guest, guest, sibling).wait_recv()
            if number == 0 and which != 1:
                for index in range(len(K_PARTS)):
                    part = kern_part(which, index)
                    pltpu.make_async_remote_copy(
                        src_ref=part, dst_ref=part, send_sem=kern_send.at[which, index], recv_sem=kern_recv.at[which, index],
                        device_id={"obs": sibling}, device_id_type=MESH,
                    ).wait_recv()
                fill_kern(which)
            profiles = jnp.concatenate([prof_ref[own, :]] + [guest_ref[guest] for guest in guests], axis=0)
            left, middle, right = profiles[:, 0:256], profiles[:, 256:512], profiles[:, 512:640]
            dot = lambda one, two: jnp.dot(one, two, preferred_element_type=F32)
            dot_turned = lambda one, two: lax.dot_general(one, two, NT, preferred_element_type=F32)
            adjoint = jnp.concatenate(
                [
                    dot(profiles, kern[which, 0:640, :]),
                    dot_turned(left, kern[which, 256:512, :]) + dot(profiles[:, 256:640], kern[which, 640:1024, :]),
                    dot_turned(left, kern[which, 512:640, :]) + dot_turned(middle, kern[which, 896:1024, :])
                    + dot(right, kern[which, 1024:1152, 0:128]),
                ],
                axis=1,
            )
            away_shift = kern[which, 1056:1072, 0:128].astype(F32)[8:9, 0:1]
            rows_out = jnp.where(iota(adjoint.shape, 1) == FEAT, away_shift, adjoint).astype(BF)
            target_ref[own, :] = rows_out[0:OBS_ROWS]
            for index, guest in enumerate(guests):
                reply_ref[guest] = rows_out[(index + 1) * OBS_ROWS : (index + 2) * OBS_ROWS]

            def answer():
                for guest in guests:
                    if guest < 3:
                        go(copy_of(number + 1, reply_ref.at[guest], target_ref.at[own], guest, guest, sibling))
                    else:
                        back = lax.rem(chip + (1 if guest == 3 else 3), N_CHIP) * 2 + (1 if guest == 3 else 0)
                        go(copy_of(number + 1, reply_ref.at[guest], target_ref.at[own], guest, 3 + core, back))

            last = after is not None and which == 2
            if not last:
                answer()
            profiles = profiles.astype(F32)
            moment += total(profiles * (adjoint + away_shift * profiles))
            if last:
                after(moment)
                answer()
        return moment

    def replies(number, target_ref):
        for slot in range(3):
            here = target_ref.at[slab(chip + slot + 3, 1 - core)]
            copy_of(number, here, here, slot, slot, sibling).wait_recv()
        for other in range(2):
            here = target_ref.at[slab(chip + 2, other)]
            copy_of(number, here, here, 3 + other, 3 + other, sibling).wait_recv()

    def whole(adj_ref, prof_ref):
        adjoint = adj_ref[...].astype(F32)
        shifts = adjoint[:, FEAT : FEAT + 1]
        return jnp.where(iota((SLOTS, FPAD), 1) < FEAT, adjoint + shifts * prof_ref[...].astype(F32), 0.0)

    gathered = jnp.dot(same[...], rows0[...], preferred_element_type=F32)
    moment0 = send_profiles(0, gathered, prof0, guest0, rows0)
    moment1 = apply_kern(0, prof0, guest0, reply0, rows1, None)
    replies(1, rows1)
    full1[...] = whole(rows1, prof0)
    high, low = halves(full1[...])
    gathered = jnp.dot(same[...], high, preferred_element_type=F32) + jnp.dot(same[...], low, preferred_element_type=F32)
    moment2 = send_profiles(2, gathered, prof1, guest1, full1)

    row = iota((8, 128), 0)
    sums = []

    def send_moments(moment3):
        tile_a[obs] = jnp.where(
            row == 0, moment0, jnp.where(row == 1, moment1, jnp.where(row == 2, moment2, jnp.where(row == 3, moment3, 0.0)))
        )
        for step in (4, 5, 3, 2, 6, 7, 1):
            copy = pltpu.make_async_remote_copy(
                src_ref=tile_a.at[obs], dst_ref=tile_a.at[obs], send_sem=sum_send.at[step], recv_sem=sum_recv.at[step],
                device_id={"obs": lax.rem(obs + step, N_OBS)}, device_id_type=MESH,
            )
            copy.start()
            sums.append(copy)

    apply_kern(2, prof1, guest1, reply1, rows2, send_moments)
    for copy in sums:
        copy.wait_recv()
    tile_b[col] = jnp.sum(tile_a[...], axis=0)
    sums_col = []
    for step, other in enumerate(plane):
        copy = pltpu.make_async_remote_copy(
            src_ref=tile_b.at[col], dst_ref=tile_b.at[col], send_sem=sum_send.at[8 + step], recv_sem=sum_recv.at[8 + step],
            device_id={"col": other}, device_id_type=MESH,
        )
        copy.start()
        sums_col.append(copy)
    replies(3, rows2)
    wide[0] = jnp.dot(rows0[...], lift_low[...], preferred_element_type=F32)
    high, low = halves(full1[...])
    wide[1] = jnp.dot(high, lift_low[...], preferred_element_type=F32) + jnp.dot(low, lift_low[...], preferred_element_type=F32)
    high, low = halves(whole(rows2, prof1))
    wide[2] = jnp.dot(high, lift_low[...], preferred_element_type=F32) + jnp.dot(low, lift_low[...], preferred_element_type=F32)
    for copy in sums_col:
        copy.wait_recv()
    moments = jnp.sum(tile_b[...], axis=0)
    m0, m1, m2, m3 = (moments[index : index + 1, 0:1] for index in range(4))

    step0 = m0 / (m0 + m1)
    rest = 1.0 - step0
    norm1 = rest * rest * m0 - 2.0 * step0 * rest * m1 + step0 * step0 * m2
    dir0, dir1 = rest + norm1 / m0, -step0
    curve = dir0 * dir0 * m0 + (dir0 * (dir0 + dir1) + dir0 * dir1) * m1 + (dir0 * dir1 + dir1 * (dir0 + dir1)) * m2 + dir1 * dir1 * m3
    step1 = norm1 / curve
    tail = iota((SLOTS, FPAD), 1) >= FEAT
    stores = [pltpu.make_async_copy(ready.at[half], out.at[half], out_sem.at[half]) for half in range(2)]
    inc = (step0 + step1 * dir0) * wide[0] + (step1 * dir1) * wide[1]
    ready[0] = jnp.where(tail, rows0[...].astype(F32), inc).astype(BF)
    stores[0].start()
    res = (rest - step1 * dir0) * wide[0] - (step0 + step1 * (dir0 + dir1)) * wide[1] - (step1 * dir1) * wide[2]
    ready[1] = jnp.where(tail, 0.0, res).astype(BF)
    stores[1].start()

    for copy in (*col_copies, *kern_copies, *sends, *sums, *sums_col):
        copy.wait_send()
    for store in stores:
        store.wait()


def expand(packed, out_inc, out_res, taken, full_inc, full_res, in_sem, out_sem):
    parts = FPAD // 128
    levels = 128 // NVAR
    order = (parts - 1, *range(parts - 1))
    loads = [
        pltpu.make_async_copy(packed.at[:, :, pl.ds(128 * part, 128)], taken.at[part], in_sem.at[part]) for part in range(parts)
    ]
    for part in order:
        loads[part].start()
    loads[parts - 1].wait()
    extra = taken[parts - 1, 0].astype(F32)
    at = FEAT - 512
    column_of = jnp.where(extra[:, at + 2 : at + 3] > 0.5, extra[:, at : at + 1] * 32.0 + extra[:, at + 1 : at + 2], -1.0)
    hit = jnp.where(column_of.astype(jnp.int32) == iota((SLOTS, COLS_DEV), 1), 1.0, 0.0).astype(BF)
    contract = (((0,), (0,)), ((), ()))
    stores = []
    for part in order:
        if part < parts - 1:
            loads[part].wait()
        count = min(levels, LEV - levels * part)
        for index, (full, out) in enumerate(((full_inc, out_inc), (full_res, out_res))):
            values = lax.dot_general(taken[part, index], hit, contract, preferred_element_type=F32)
            full[levels * part : levels * part + count] = values[0 : NVAR * count].reshape(count, NVAR, COLS_DEV)
            here = pl.ds(levels * part, count)
            store = pltpu.make_async_copy(full.at[here], out.at[here], out_sem.at[part, index])
            store.start()
            stores.append(store)
    for store in stores:
        store.wait()


def per_device(departures, obs_owner, obs_column, obs_count, channel_count, error_inv, jacobian, vertical):
    vmem, hbm = pl.BlockSpec(memory_space=pltpu.VMEM), pl.BlockSpec(memory_space=pltpu.HBM)
    dma = pltpu.SemaphoreType.DMA
    slab = pltpu.VMEM((SLOTS, FPAD), BF)
    packed = pl.pallas_call(
        inner_loop,
        out_shape=jax.ShapeDtypeStruct((2, SLOTS, FPAD), BF),
        in_specs=[hbm] * 8,
        out_specs=hbm,
        scratch_shapes=[
            pltpu.SMEM((1,), jnp.int32),
            pltpu.SMEM((1,), jnp.int32),
            pltpu.VMEM((1, ROWS), jnp.int32),
            pltpu.VMEM((1, ROWS), jnp.int32),
            pltpu.VMEM((1, CH), F32),
            pltpu.VMEM((LEV, NVAR, LEV), F32),
            pltpu.VMEM((NCHUNK, ROWS, CHUNK), F32),
            pltpu.VMEM((NCHUNK, FEAT, CHUNK), BF),
            pltpu.VMEM((FPAD, NVAR * 256), F32),
            pltpu.VMEM((FPAD, FPAD), BF),
            pltpu.VMEM((FPAD, FPAD), F32),
            pltpu.VMEM((FPAD, FPAD), BF),
            pltpu.VMEM((3, K_ROWS, 256), BF),
            pltpu.VMEM((FPAD, 256), F32),
            pltpu.VMEM((SLOTS, SLOTS), BF),
            pltpu.VMEM((SLOTS, FPAD), F32),
            pltpu.VMEM((3, SLOTS, FPAD), F32),
            pltpu.VMEM((2, SLOTS, FPAD), BF),
            *([slab] * 8),
            *([pltpu.VMEM((GUESTS, OBS_ROWS, FPAD), BF)] * 4),
            pltpu.VMEM((N_OBS, 8, 128), F32),
            pltpu.VMEM((N_COL, 8, 128), F32),
            dma((2, NCHUNK)),
            dma((6,)),
            dma((N_COL,)),
            dma((N_COL,)),
            dma((1, N_OBS)),
            dma((1, N_OBS)),
            dma((3, len(K_PARTS))),
            dma((3, len(K_PARTS))),
            dma((4, GUESTS)),
            dma((4, GUESTS)),
            dma((24,)),
            dma((24,)),
            pltpu.VMEM((2, SLOTS, FPAD), BF),
            dma((2,)),
        ],
        compiler_params=pltpu.CompilerParams(collective_id=0, has_side_effects=True, vmem_limit_bytes=62 << 20),
        name="inner_loop",
    )(
        obs_count, channel_count, obs_owner.reshape(1, ROWS), obs_column.reshape(1, ROWS), error_inv,
        vertical.transpose(1, 0, 2), departures, jacobian,
    )
    out = jax.ShapeDtypeStruct((LEV, NVAR, COLS_DEV), F32)
    inc, res = pl.pallas_call(
        expand,
        out_shape=(out, out),
        in_specs=[hbm],
        out_specs=(hbm, hbm),
        scratch_shapes=[
            pltpu.VMEM((FPAD // 128, 2, SLOTS, 128), BF),
            pltpu.VMEM((LEV, NVAR, COLS_DEV), F32),
            pltpu.VMEM((LEV, NVAR, COLS_DEV), F32),
            dma((FPAD // 128,)),
            dma((FPAD // 128, 2)),
        ],
        compiler_params=pltpu.CompilerParams(vmem_limit_bytes=62 << 20),
        name="expand",
    )(packed)
    return inc.transpose(1, 0, 2), res.transpose(1, 0, 2)


def solution(mesh):
    in_specs = (
        P(("col", "obs"), None),
        P(("col", "obs"), None),
        P(("col", "obs")),
        P(("col", "obs")),
        P("obs"),
        P("obs", None),
        P("obs", None, None),
        P(),
    )
    out_specs = (P(None, None, ("col", "obs")), P(None, None, ("col", "obs")))
    return jax.shard_map(per_device, mesh=mesh, in_specs=in_specs, out_specs=out_specs, check_vma=False)
```
